1024 devices in a mesh: cl: 128 (over z, x, core), grp: 8 (over y).
Axes of the slice: x: 8, y: 8, z: 8, core: 2. Of those that a mesh axis runs over, the one named last changes fastest.
Arguments:
- basis: float32 [16, 8, 1024, 128], P(None, 'grp', 'cl'), may hold values from -6 to 6
- near_blocks: bfloat16 [8, 1024, 4, 128, 128], P('grp', 'cl'), may hold values from -0.25 to 0.25
- near_list: int32 [8, 1024, 4], P('grp', 'cl'), may hold values from 0 to 23
- source_basis: bfloat16 [8, 1024, 32, 128], P('grp', 'cl'), may hold values from -0.5 to 0.5
- target_basis: bfloat16 [8, 1024, 32, 128], P('grp', 'cl'), may hold values from -1 to 1
- coupling: bfloat16 [8, 2048, 1024], P('grp', 'cl'), may hold values from -0.75 to 0.75
- far_target: int32 [8, 2048], P('grp'), may hold values from 0 to 1023, as said below
- far_source: int32 [8, 2048], P('grp', 'cl'), may hold values from 0 to 1023, as said below
- far_count: int32 [8, 128], P('grp', 'cl'), may hold values from 8 to 16
Outputs:
- next_vector: float32 [8, 1024, 128], P('grp', 'cl')
- hessenberg: float32 [17], replicated
The draws below stay inside these ranges and needn't reach their ends.
Inputs may be any that keep to these rules, and one draw needn't show every extreme that they name: `far_target`: slots are owned in blocks of 16, block d by owner d of the group, whose clusters are d * 8 to (d + 1) * 8 - 1. Except for slot 1 of each owner, a slot's target lies within 16 clusters before or 23 after the owner's first cluster. Slot 1's target is a cluster of owner (d + 64) % 128. `far_source`: except for slot 0 of each owner, a slot's source lies within 80 clusters before or 87 after the owner's first cluster, and where the slot's target obeys the rule above the source differs from it by 16 to 64 clusters. Slot 0's source is a cluster of owner (d + 64) % 128.
All inputs are finite; a program needn't handle non-finite values.
Results may differ from the reference program's by a relative error of at most 0.0039.
Values may be sent and summed in bfloat16 or wider, within the bound.
No kernel may reach another device: no remote copies, remote signals or barrier semaphores. Data moves between devices by JAX's collectives and lax.ppermute only.
A program may use at most 32 MiB of HBM per device.

```python
import jax
import jax.numpy as jnp
from jax import lax

P_SIZE = 128
R = 32
CL_DEV = 8
NEAR_K = 4
FAR_DEV = 16
K = 16
CLUSTERS_GRP = 1024
PANELS = 1048576
N_CL = 128
N_GRP = 8


def far_pairs(key):
    slot_total = N_CL * FAR_DEV
    shape = (N_GRP, slot_total)
    slot_ids = jnp.arange(slot_total, dtype=jnp.int32)
    owner = (slot_ids // FAR_DEV)[None, :]
    local_slot = (slot_ids % FAR_DEV)[None, :]
    key_target = jax.random.fold_in(key, 101)
    key_offset = jax.random.fold_in(key, 202)
    key_sign = jax.random.fold_in(key, 303)
    key_remote = jax.random.fold_in(key, 404)
    target = owner * CL_DEV + jax.random.randint(key_target, shape, -2 * CL_DEV, 3 * CL_DEV, dtype=jnp.int32)
    target = jnp.clip(target, 0, CLUSTERS_GRP - 1)
    reach = min(8 * CL_DEV, CLUSTERS_GRP // 2)
    offset = jax.random.randint(key_offset, shape, 2 * CL_DEV, reach + 1, dtype=jnp.int32)
    direction = jax.random.randint(key_sign, shape, 0, 2, dtype=jnp.int32) * 2 - 1
    upward = target + direction * offset
    source = jnp.where((upward >= 0) & (upward < CLUSTERS_GRP), upward, target - direction * offset)
    opposite = (owner + N_CL // 2) % N_CL * CL_DEV + jax.random.randint(key_remote, shape, 0, CL_DEV, dtype=jnp.int32)
    source = jnp.where(local_slot == 0, opposite, source)
    target = jnp.where(local_slot == 1, opposite, target)
    return (target.astype(jnp.int32), source.astype(jnp.int32))


def draw_far_target(key, part):
    return far_pairs(key)[0]


def draw_far_source(key, part):
    return far_pairs(key)[1]


def plant(result, rng, least, top_value):
    extent = result.shape
    spot = [jax.random.randint(jax.random.fold_in(rng, axis), (), 0, extent[axis]) for axis in range(len(extent))]
    result = result.at[tuple(spot)].set(least)
    longest = extent.index(max(extent))
    spot[longest] = (spot[longest] + 1) % extent[longest]
    return result.at[tuple(spot)].set(top_value)


def block_levels(key, extent, shards, least, top_value):
    def one(position, parts):
        draws = jax.random.uniform(jax.random.fold_in(jax.random.fold_in(key, 6), position), (parts,), jnp.float32, least / len(shards), top_value / len(shards))
        return jnp.repeat(jnp.exp(draws), extent[position] // parts).reshape((-1,) + (1,) * (len(extent) - position - 1))

    gain = one(*shards[0])
    for cut in shards[1:]:
        gain = gain * one(*cut)
    return gain


def gaussian(rng, dims, spread, most, pieces=(), held_as=jnp.bfloat16):
    gain = block_levels(rng, dims, pieces, -0.22, 0.18) if pieces else 1.0
    drawn = jax.random.normal(rng, dims, jnp.float32) * spread * gain
    return jnp.minimum(jnp.maximum(drawn, -most), most).astype(held_as)


def setup_inputs(seed: int = 0) -> dict:
    keys = jax.random.split(jax.random.key(seed), 10)
    return {
        "basis": gaussian(keys[0], (K, N_GRP, CLUSTERS_GRP, P_SIZE), 1.0, 6.0, ((1, 8), (2, 128)), jnp.float32),
        "near_blocks": gaussian(keys[1], (N_GRP, CLUSTERS_GRP, NEAR_K, P_SIZE, P_SIZE), (NEAR_K * P_SIZE) ** -0.5, 0.25, ((0, 8), (1, 128))),
        "near_list": plant(jax.random.randint(keys[2], (N_GRP, CLUSTERS_GRP, NEAR_K), 0, 3 * CL_DEV), jax.random.fold_in(keys[2], 1), 0, (3 * CL_DEV) - 1).astype(jnp.int32),
        "source_basis": gaussian(keys[3], (N_GRP, CLUSTERS_GRP, R, P_SIZE), P_SIZE ** -0.5, 0.5, ((0, 8), (1, 128))),
        "target_basis": gaussian(keys[4], (N_GRP, CLUSTERS_GRP, R, P_SIZE), R ** -0.5, 1.0, ((0, 8), (1, 128))),
        "coupling": gaussian(keys[5], (N_GRP, N_CL * FAR_DEV, R * R), (R * max(1, FAR_DEV // CL_DEV)) ** -0.5, 0.75, ((0, 8), (1, 128))),
        "far_target": draw_far_target(jax.random.fold_in(keys[9], 71), 0),
        "far_source": draw_far_source(jax.random.fold_in(keys[9], 71), 0),
        "far_count": plant(jax.random.randint(keys[8], (N_GRP, N_CL), FAR_DEV // 2, FAR_DEV + 1), jax.random.fold_in(keys[8], 1), FAR_DEV // 2, FAR_DEV).astype(jnp.int32),
    }


def group_image(packed):
    current_bf, current, blocks, near_ids, sbasis, tbasis, couplings, targets, sources, counts = packed
    padded = jnp.pad(current_bf, ((CL_DEV, CL_DEV), (0, 0)))
    window_start = jnp.arange(CLUSTERS_GRP, dtype=jnp.int32) // CL_DEV * CL_DEV
    source_rows = window_start[:, None] + near_ids.astype(jnp.int32)
    gathered = padded[source_rows]
    near_part = jnp.einsum('tkij,tkj->ti', blocks.astype(jnp.float32), gathered.astype(jnp.float32), precision=lax.Precision.HIGHEST)
    expansion = jnp.einsum('srp,sp->sr', sbasis.astype(jnp.float32), current_bf.astype(jnp.float32), precision=lax.Precision.HIGHEST).astype(jnp.bfloat16)
    slot_index = jnp.arange(N_CL * FAR_DEV, dtype=jnp.int32)
    live_mask = (slot_index % FAR_DEV < counts[slot_index // FAR_DEV]).astype(jnp.float32)
    square_blocks = couplings.reshape(N_CL * FAR_DEV, R, R).astype(jnp.float32)
    term = jnp.einsum('bij,bj->bi', square_blocks, expansion[sources].astype(jnp.float32), precision=lax.Precision.HIGHEST) * live_mask[:, None]
    coupled = jnp.zeros((CLUSTERS_GRP, R), jnp.float32).at[targets].add(term).astype(jnp.bfloat16)
    far_part = jnp.einsum('tr,trp->tp', coupled.astype(jnp.float32), tbasis.astype(jnp.float32), precision=lax.Precision.HIGHEST)
    return 0.5 * current + near_part + far_part

def reference(basis, near_blocks, near_list, source_basis, target_basis, coupling, far_target, far_source, far_count):
    current = basis[K - 1]
    current_bf = current.astype(jnp.bfloat16)
    image = lax.map(group_image, (current_bf, current, near_blocks, near_list, source_basis, target_basis, coupling, far_target, far_source, far_count))
    flat_basis = basis.reshape(K, -1)
    flat_image = image.reshape(-1)
    projection = jnp.dot(flat_basis, flat_image, precision=lax.Precision.HIGHEST) / PANELS
    remainder = flat_image - jnp.dot(projection, flat_basis, precision=lax.Precision.HIGHEST)
    new_norm = jnp.sqrt(jnp.sum(remainder * remainder) / PANELS + 1e-06)
    next_vector = (remainder / new_norm).reshape(image.shape)
    return (next_vector, jnp.concatenate([projection, new_norm[None]]))
```

```python
import jax
import jax.numpy as jnp
from jax import lax
from jax.sharding import Mesh
from jax.sharding import PartitionSpec as P

CL = ("z", "x", "core")
ROW = ("x", "core")
COLUMN = ("z", "grp")
HIGHEST = lax.Precision.HIGHEST


def neighbour(value, step):
    count = lax.axis_size(CL)
    route = [(i, i + step) for i in range(count) if 0 <= i + step < count]
    return lax.ppermute(value, CL, route)


def exchange(rows, axes):
    return lax.all_to_all(rows, axes, 0, 0, tiled=True)


def summed(row, axes):
    sent = jnp.broadcast_to(row, (lax.axis_size(axes), row.shape[1]))
    return jnp.sum(exchange(sent, axes), axis=0, keepdims=True)


def on_device(
    basis,
    near_blocks,
    near_list,
    source_basis,
    target_basis,
    coupling,
    far_target,
    far_source,
    far_count,
):
    basis_count = basis.shape[0]
    clusters = basis.shape[2]
    panels_cl = basis.shape[3]
    ranks = source_basis.shape[2]
    slots = coupling.shape[1]
    owners = lax.axis_size(CL)
    me = lax.axis_index(CL)
    current = basis[basis_count - 1, 0]
    current_bf = current.astype(jnp.bfloat16)
    before = neighbour(current_bf, 1)
    after = neighbour(current_bf, -1)
    expansion = jnp.einsum(
        "srp,sp->sr", source_basis[0], current_bf, preferred_element_type=jnp.float32
    ).astype(jnp.bfloat16)
    row = expansion.astype(jnp.float32).reshape(1, clusters * ranks)
    everyone = exchange(jnp.broadcast_to(row, (owners, clusters * ranks)), CL)
    picked = everyone.reshape(owners * clusters, ranks)[far_source[0]].astype(jnp.bfloat16)
    slot = jnp.arange(slots, dtype=jnp.int32)
    live = (slot < far_count[0, 0]).astype(jnp.float32)
    term = (
        jnp.einsum(
            "bij,bj->bi",
            coupling[0].reshape(slots, ranks, ranks),
            picked,
            preferred_element_type=jnp.float32,
        )
        * live[:, None]
    )
    targets = lax.dynamic_slice_in_dim(far_target[0], me * slots, slots)
    selector = jnp.arange(owners * clusters, dtype=jnp.int32)[:, None] == targets[None, :]
    sums = jnp.dot(selector.astype(jnp.float32), term, precision=HIGHEST)
    arrived = exchange(sums.reshape(owners, clusters * ranks), CL)
    coupled = jnp.sum(arrived, axis=0).reshape(clusters, ranks).astype(jnp.bfloat16)
    far_part = jnp.einsum(
        "tr,trp->tp", coupled, target_basis[0], preferred_element_type=jnp.float32
    )
    window = jnp.concatenate([before, current_bf, after], axis=0)
    near_part = jnp.einsum(
        "tkij,tkj->ti", near_blocks[0], window[near_list[0]], preferred_element_type=jnp.float32
    )
    image = (0.5 * current + near_part + far_part).reshape(1, -1)
    flat_basis = basis[:, 0].reshape(basis_count, clusters * panels_cl)
    both = jnp.concatenate([flat_basis, image], axis=0)
    inner = jnp.dot(both, both.T, precision=HIGHEST)
    packed = jnp.concatenate([inner[k : k + 1] for k in range(basis_count + 1)], axis=1)
    total = summed(summed(packed, ROW), COLUMN).reshape(basis_count + 1, basis_count + 1)
    panels = float(owners * lax.axis_size("grp") * clusters * panels_cl)
    products = total[basis_count, :basis_count]
    gram = total[:basis_count, :basis_count]
    projection = products / panels
    remainder = image[0] - jnp.dot(projection, flat_basis, precision=HIGHEST)
    squares = (
        total[basis_count, basis_count]
        - 2.0 * jnp.sum(projection * products)
        + jnp.sum(projection * jnp.sum(gram * projection[None, :], axis=1))
    )
    new_norm = jnp.sqrt(squares / panels + 1e-06)
    next_vector = (remainder / new_norm).reshape(1, clusters, panels_cl)
    return (next_vector, jnp.concatenate([projection, new_norm[None]]))


def solution(mesh):
    torus = Mesh(mesh.devices.reshape(8, 8, 2, mesh.shape["grp"]), (*CL, "grp"))
    in_specs = (
        P(None, "grp", CL, None),
        P("grp", CL, None, None, None),
        P("grp", CL, None),
        P("grp", CL, None, None),
        P("grp", CL, None, None),
        P("grp", CL, None),
        P("grp", None),
        P("grp", CL),
        P("grp", CL),
    )
    return jax.shard_map(
        on_device,
        mesh=torus,
        in_specs=in_specs,
        out_specs=(P("grp", CL, None), P()),
        check_vma=False,
    )
```

```python
import jax
import jax.numpy as jnp
from jax import lax
from jax.experimental import pallas as pl
from jax.experimental.pallas import tpu as pltpu
from jax.sharding import Mesh
from jax.sharding import PartitionSpec as P

CL = ("z", "x", "core")
ROW = ("x", "core")
COLUMN = ("z", "grp")
HIGHEST = lax.Precision.HIGHEST
LANES = 128
FIRST, LAST = -2, 3

SMALL = pltpu.CompilerParams(vmem_limit_bytes=4 * 1024 * 1024)
VMEM = pl.BlockSpec(memory_space=pltpu.VMEM)
SMEM = pl.BlockSpec(memory_space=pltpu.SMEM)


def iota(shape, dim):
    return lax.broadcasted_iota(jnp.int32, shape, dim)


def dot(a, b, contract=((1,), (0,)), precision=None):
    return lax.dot_general(
        a, b, (contract, ((), ())), precision=precision, preferred_element_type=jnp.float32
    )


def ones_where(mask, dtype):
    return jnp.where(mask, 1.0, 0.0).astype(dtype)


def position():
    return lax.axis_index("z") * 16 + lax.axis_index("x") * 2 + lax.axis_index("core")


def expand_kernel(basis_ref, source_ref, sent_ref, current_ref):
    current = basis_ref[0, 0].astype(jnp.bfloat16)
    current_ref[...] = current
    clusters, panels = current.shape
    ranks = source_ref.shape[2]
    width = clusters * ranks
    source = source_ref[0].reshape(width, panels)
    every = dot(current, source, ((1,), (1,)))
    own = iota((clusters, width), 1) // ranks == iota((clusters, width), 0)
    row = jnp.sum(jnp.where(own, every, 0.0), axis=0, keepdims=True)
    row = row.astype(jnp.bfloat16).astype(jnp.float32)
    sent_ref[...] = jnp.broadcast_to(row[None], sent_ref.shape)


def far_kernel(
    clusters, owners, source_ref, target_ref, count_ref, expansion_ref, coupling_ref, sent_ref
):
    slots = coupling_ref.shape[1]
    width = expansion_ref.shape[2]
    ranks = width // clusters
    groups = LANES // ranks
    parts = ranks // groups
    me = position()
    lane_cluster = iota((1, width), 1) // ranks
    picked, targets = [], []
    for b in range(slots):
        source = source_ref[0, b]
        row = expansion_ref[source // clusters]
        picked.append(jnp.where(lane_cluster == source % clusters, row, 0.0))
        target = jnp.where(b < count_ref[0, 0], target_ref[0, b], -1)
        targets.append(jnp.full((1, width), target, jnp.int32))
    picked = jnp.concatenate(picked, axis=0).astype(jnp.bfloat16)
    targets = jnp.concatenate(targets, axis=0)
    spread = iota((width, LANES), 0) % ranks == iota((width, LANES), 1) % ranks
    vector = dot(picked, ones_where(spread, jnp.bfloat16))
    coupling = coupling_ref[0].astype(jnp.float32)
    high, low = [], []
    for q in range(parts):
        product = coupling[:, q * LANES : (q + 1) * LANES] * vector
        top = product.astype(jnp.bfloat16)
        high.append(top)
        low.append((product - top.astype(jnp.float32)).astype(jnp.bfloat16))
    gather = iota((LANES, width), 0) // ranks == iota((LANES, width), 1) % groups
    sums = dot(jnp.concatenate(high + low, axis=0), ones_where(gather, jnp.bfloat16))
    part = (iota((slots, width), 1) % ranks) // groups
    term = jnp.zeros((slots, width), jnp.float32)
    for q in range(parts):
        value = sums[q * slots : (q + 1) * slots] + sums[(parts + q) * slots : (parts + q + 1) * slots]
        term = jnp.where(part == q, value, term)
    sent_ref[...] = jnp.zeros_like(sent_ref)

    def send(owner):
        mine = targets == owner * clusters + lane_cluster
        sent_ref[owner] = jnp.sum(jnp.where(mine, term, 0.0), axis=0, keepdims=True)

    for step in range(FIRST, LAST + 1):
        owner = me + step

        @pl.when(jnp.logical_and(owner >= 0, owner < owners))
        def _():
            send(owner)

    send(lax.rem(me + owners // 2, owners))


def gram_kernel(basis_ref, gram_ref):
    count, _, clusters, _ = basis_ref.shape
    gram = jnp.zeros((count, count), jnp.float32)
    for c in range(clusters):
        rows = basis_ref[:, 0, c, :]
        gram = gram + dot(rows, rows, ((1,), (1,)), HIGHEST)
    width = count * count
    tile = iota((count, width), 1) % count == iota((count, width), 0)
    rows = dot(gram, ones_where(tile, jnp.float32), precision=HIGHEST)
    own = iota((count, width), 1) // count == iota((count, width), 0)
    gram_ref[...] = jnp.sum(jnp.where(own, rows, 0.0), axis=0, keepdims=True)


def image_kernel(owners, basis_ref, target_ref, arrived_ref, near_ref, gram_ref, image_ref, sent_ref):
    count = basis_ref.shape[0]
    clusters, panels = near_ref.shape
    ranks = target_ref.shape[2]
    width = clusters * ranks
    me = position()
    coupled = arrived_ref[lax.rem(me + owners // 2, owners)]
    for step in range(-LAST, -FIRST + 1):
        owner = me + step
        inside = jnp.logical_and(owner >= 0, owner < owners)
        value = arrived_ref[jnp.clip(owner, 0, owners - 1)]
        coupled = coupled + jnp.where(inside, value, 0.0)
    own = iota((clusters, width), 1) // ranks == iota((clusters, width), 0)
    spread = jnp.where(own, coupled, 0.0).astype(jnp.bfloat16)
    far = dot(spread, target_ref[0].reshape(width, panels))
    image = 0.5 * basis_ref[count - 1, 0] + near_ref[...] + far
    image_ref[...] = image
    rows = [jnp.sum(basis_ref[k, 0] * image, axis=0, keepdims=True) for k in range(count)]
    rows.append(jnp.sum(image * image, axis=0, keepdims=True))
    rows.append(jnp.zeros((LANES - count - 1, panels), jnp.float32))
    products = dot(
        jnp.ones((8, panels), jnp.float32), jnp.concatenate(rows, axis=0), ((1,), (1,)), HIGHEST
    )
    row = jnp.concatenate([gram_ref[...], products[:1]], axis=1)
    sent_ref[...] = jnp.broadcast_to(row[None], sent_ref.shape)


def total_kernel(arrived_ref, sent_ref):
    sent_ref[...] = jnp.broadcast_to(
        jnp.sum(arrived_ref[...], axis=0, keepdims=True), sent_ref.shape
    )


def final_kernel(all_panels, basis_ref, image_ref, arrived_ref, next_ref, hessenberg_ref):
    count = basis_ref.shape[0]
    width = count * count
    total = jnp.sum(arrived_ref[...], axis=0)
    gram = total[:, :width]
    products = total[:, width:]
    lane = iota((1, LANES), 1)
    projection = jnp.where(lane < count, products / all_panels, 0.0)
    square = jnp.sum(jnp.where(lane == count, products, 0.0), axis=1, keepdims=True)
    index = iota((LANES, width), 1)
    which = iota((LANES, width), 0)
    many = jnp.broadcast_to(projection, (8, LANES))
    outer = dot(many, ones_where(index // count == which, jnp.float32), precision=HIGHEST)
    inner = dot(many, ones_where(index % count == which, jnp.float32), precision=HIGHEST)
    squares = (
        square
        - 2.0 * jnp.sum(projection * products, axis=1, keepdims=True)
        + jnp.sum(gram * outer[:1] * inner[:1], axis=1, keepdims=True)
    )
    new_norm = jnp.sqrt(squares / all_panels + 1e-06)
    remainder = image_ref[...]
    for k in range(count):
        remainder = remainder - projection[:, k : k + 1] * basis_ref[k, 0]
    next_ref[0] = remainder / new_norm
    column = jnp.where(lane == count, new_norm, projection)
    hessenberg_ref[...] = column[:, : count + 1]


def exchange(rows, axes):
    return lax.all_to_all(rows, axes, 0, 0)


def neighbour(value, step):
    count = lax.axis_size(CL)
    route = [(i, i + step) for i in range(count) if 0 <= i + step < count]
    return lax.ppermute(value, CL, route)


def f32(*shape):
    return jax.ShapeDtypeStruct(shape, jnp.float32)


def on_device(
    basis,
    near_blocks,
    near_list,
    source_basis,
    target_basis,
    coupling,
    far_target,
    far_source,
    far_count,
):
    count, _, clusters, panels = basis.shape
    ranks = source_basis.shape[2]
    slots = coupling.shape[1]
    owners = lax.axis_size(CL)
    width = clusters * ranks
    packed = count * count + LANES

    sent, current = pl.pallas_call(
        expand_kernel,
        grid=(1,),
        in_specs=[
            pl.BlockSpec((1, 1, clusters, panels), lambda i: (count - 1, 0, 0, 0)),
            pl.BlockSpec(source_basis.shape, lambda i: (0, 0, 0, 0)),
        ],
        out_specs=[
            pl.BlockSpec((owners, 1, width), lambda i: (0, 0, 0)),
            pl.BlockSpec((clusters, panels), lambda i: (0, 0)),
        ],
        out_shape=[f32(owners, 1, width), jax.ShapeDtypeStruct((clusters, panels), jnp.bfloat16)],
        name="expand",
    )(basis, source_basis)
    expansions = exchange(sent, CL)
    before = neighbour(current, 1)
    after = neighbour(current, -1)

    me = lax.axis_index(CL)
    targets = lax.dynamic_slice_in_dim(far_target, me * slots, slots, axis=1)
    sent = pl.pallas_call(
        lambda *refs: far_kernel(clusters, owners, *refs),
        in_specs=[SMEM, SMEM, SMEM, VMEM, VMEM],
        out_specs=VMEM,
        out_shape=f32(owners, 1, width),
        compiler_params=SMALL,
        name="far",
    )(far_source, targets, far_count, expansions, coupling)
    arrived = exchange(sent, CL)

    window = jnp.concatenate([before, current, after], axis=0)
    near = jnp.einsum(
        "tkij,tkj->ti", near_blocks[0], window[near_list[0]], preferred_element_type=jnp.float32
    )
    gram = pl.pallas_call(
        gram_kernel, in_specs=[VMEM], out_specs=VMEM, out_shape=f32(1, count * count), compiler_params=SMALL, name="gram"
    )(basis)
    image, sent = pl.pallas_call(
        lambda *refs: image_kernel(owners, *refs),
        in_specs=[VMEM] * 5,
        out_specs=[VMEM] * 2,
        out_shape=[f32(clusters, panels), f32(lax.axis_size(ROW), 1, packed)],
        compiler_params=SMALL,
        name="image",
    )(basis, target_basis, arrived, near, gram)
    sent = pl.pallas_call(
        total_kernel,
        in_specs=[VMEM],
        out_specs=VMEM,
        out_shape=f32(lax.axis_size(COLUMN), 1, packed),
        compiler_params=SMALL,
        name="total",
    )(exchange(sent, ROW))
    all_panels = float(owners * lax.axis_size("grp") * clusters * panels)
    next_vector, hessenberg = pl.pallas_call(
        lambda *refs: final_kernel(all_panels, *refs),
        in_specs=[VMEM] * 3,
        out_specs=[VMEM] * 2,
        out_shape=[f32(1, clusters, panels), f32(1, count + 1)],
        compiler_params=SMALL,
        name="final",
    )(basis, image, exchange(sent, COLUMN))
    return (next_vector, hessenberg.reshape(count + 1))


def solution(mesh):
    torus = Mesh(mesh.devices.reshape(8, 8, 2, mesh.shape["grp"]), (*CL, "grp"))
    in_specs = (
        P(None, "grp", CL, None),
        P("grp", CL, None, None, None),
        P("grp", CL, None),
        P("grp", CL, None, None),
        P("grp", CL, None, None),
        P("grp", CL, None),
        P("grp", None),
        P("grp", CL),
        P("grp", CL),
    )
    return jax.shard_map(
        on_device,
        mesh=torus,
        in_specs=in_specs,
        out_specs=(P("grp", CL, None), P()),
        check_vma=False,
    )
```

```python
import jax
import jax.numpy as jnp
from jax import lax
from jax.experimental import pallas as pl
from jax.experimental.pallas import tpu as pltpu
from jax.sharding import Mesh
from jax.sharding import PartitionSpec as P

CL = ("z", "x", "core")
ROW = ("x", "core")
COLUMN = ("z", "grp")
HIGHEST = lax.Precision.HIGHEST
LANES = 128
FIRST, LAST = -2, 3

SMALL = pltpu.CompilerParams(vmem_limit_bytes=4 * 1024 * 1024)
VMEM = pl.BlockSpec(memory_space=pltpu.VMEM)
SMEM = pl.BlockSpec(memory_space=pltpu.SMEM)


def iota(shape, dim):
    return lax.broadcasted_iota(jnp.int32, shape, dim)


def dot(a, b, contract=((1,), (0,)), precision=None):
    return lax.dot_general(
        a, b, (contract, ((), ())), precision=precision, preferred_element_type=jnp.float32
    )


def ones_where(mask, dtype):
    return jnp.where(mask, 1.0, 0.0).astype(dtype)


def position():
    return lax.axis_index("z") * 16 + lax.axis_index("x") * 2 + lax.axis_index("core")


def current_kernel(basis_ref, after_ref, current_ref):
    current_ref[...] = basis_ref[0, 0].astype(jnp.bfloat16)


def expand_kernel(basis_ref, source_ref, sent_ref):
    current = basis_ref[0, 0].astype(jnp.bfloat16)
    clusters, panels = current.shape
    ranks = source_ref.shape[2]
    width = clusters * ranks
    source = source_ref[0].reshape(width, panels)
    every = dot(current, source, ((1,), (1,)))
    own = iota((clusters, width), 1) // ranks == iota((clusters, width), 0)
    row = jnp.sum(jnp.where(own, every, 0.0), axis=0, keepdims=True)
    pieces = [row[:, i : i + LANES] for i in range(0, width, LANES)]
    tile = jnp.concatenate(pieces, axis=0).astype(jnp.bfloat16)
    sent_ref[...] = jnp.broadcast_to(tile[None], sent_ref.shape)


def far_kernel(
    clusters, owners, source_ref, target_ref, count_ref, expansion_ref, coupling_ref, sent_ref
):
    slots = coupling_ref.shape[1]
    width = sent_ref.shape[2]
    ranks = width // clusters
    groups = LANES // ranks
    parts = ranks // groups
    me = position()
    lane_cluster = iota((1, width), 1) // ranks
    tile = expansion_ref.shape[1:]
    place = iota(tile, 0) * groups + iota(tile, 1) // ranks
    picked, targets = [], []
    for b in range(slots):
        source = source_ref[0, b]
        rows = expansion_ref[source // clusters].astype(jnp.float32)
        rows = jnp.where(place == source % clusters, rows, 0.0)
        picked.append(jnp.sum(rows, axis=0, keepdims=True))
        target = jnp.where(b < count_ref[0, 0], target_ref[0, b], -1)
        targets.append(jnp.full((1, width), target, jnp.int32))
    picked = jnp.concatenate(picked, axis=0).astype(jnp.bfloat16)
    targets = jnp.concatenate(targets, axis=0)
    spread = iota((LANES, LANES), 0) % ranks == iota((LANES, LANES), 1) % ranks
    vector = dot(picked, ones_where(spread, jnp.bfloat16))
    coupling = coupling_ref[0].astype(jnp.float32)
    high, low = [], []
    for q in range(parts):
        product = coupling[:, q * LANES : (q + 1) * LANES] * vector
        top = product.astype(jnp.bfloat16)
        high.append(top)
        low.append((product - top.astype(jnp.float32)).astype(jnp.bfloat16))
    gather = iota((LANES, width), 0) // ranks == iota((LANES, width), 1) % groups
    sums = dot(jnp.concatenate(high + low, axis=0), ones_where(gather, jnp.bfloat16))
    part = (iota((slots, width), 1) % ranks) // groups
    term = jnp.zeros((slots, width), jnp.float32)
    for q in range(parts):
        value = sums[q * slots : (q + 1) * slots] + sums[(parts + q) * slots : (parts + q + 1) * slots]
        term = jnp.where(part == q, value, term)
    sent_ref[...] = jnp.zeros_like(sent_ref)

    def send(owner):
        mine = targets == owner * clusters + lane_cluster
        sent_ref[owner] = jnp.sum(jnp.where(mine, term, 0.0), axis=0, keepdims=True)

    for step in range(FIRST, LAST + 1):
        owner = me + step

        @pl.when(jnp.logical_and(owner >= 0, owner < owners))
        def _():
            send(owner)

    send(lax.rem(me + owners // 2, owners))


def gram_kernel(basis_ref, gram_ref):
    count, _, clusters, _ = basis_ref.shape
    gram = jnp.zeros((count, count), jnp.float32)
    for c in range(clusters):
        rows = basis_ref[:, 0, c, :]
        gram = gram + dot(rows, rows, ((1,), (1,)), HIGHEST)
    width = count * count
    tile = iota((count, width), 1) % count == iota((count, width), 0)
    rows = dot(gram, ones_where(tile, jnp.float32), precision=HIGHEST)
    own = iota((count, width), 1) // count == iota((count, width), 0)
    gram_ref[...] = jnp.sum(jnp.where(own, rows, 0.0), axis=0, keepdims=True)


def image_kernel(owners, basis_ref, target_ref, arrived_ref, near_ref, gram_ref, image_ref, sent_ref):
    count = basis_ref.shape[0]
    clusters, panels = near_ref.shape
    ranks = target_ref.shape[2]
    width = clusters * ranks
    me = position()
    coupled = arrived_ref[lax.rem(me + owners // 2, owners)]
    for step in range(-LAST, -FIRST + 1):
        owner = me + step
        inside = jnp.logical_and(owner >= 0, owner < owners)
        value = arrived_ref[jnp.clip(owner, 0, owners - 1)]
        coupled = coupled + jnp.where(inside, value, 0.0)
    own = iota((clusters, width), 1) // ranks == iota((clusters, width), 0)
    spread = jnp.where(own, coupled, 0.0).astype(jnp.bfloat16)
    far = dot(spread, target_ref[0].reshape(width, panels))
    image = 0.5 * basis_ref[count - 1, 0] + near_ref[...] + far
    image_ref[...] = image
    rows = [jnp.sum(basis_ref[k, 0] * image, axis=0, keepdims=True) for k in range(count)]
    rows.append(jnp.sum(image * image, axis=0, keepdims=True))
    rows.append(jnp.zeros((LANES - count - 1, panels), jnp.float32))
    products = dot(
        jnp.ones((8, panels), jnp.float32), jnp.concatenate(rows, axis=0), ((1,), (1,)), HIGHEST
    )
    row = jnp.concatenate([gram_ref[...], products[:1]], axis=1)
    sent_ref[...] = jnp.broadcast_to(row[None], sent_ref.shape)


def total_kernel(arrived_ref, sent_ref):
    sent_ref[...] = jnp.broadcast_to(
        jnp.sum(arrived_ref[...], axis=0, keepdims=True), sent_ref.shape
    )


def final_kernel(all_panels, basis_ref, image_ref, arrived_ref, next_ref, hessenberg_ref):
    count = basis_ref.shape[0]
    width = count * count
    total = jnp.sum(arrived_ref[...], axis=0)
    gram = total[:, :width]
    products = total[:, width:]
    lane = iota((1, LANES), 1)
    projection = jnp.where(lane < count, products / all_panels, 0.0)
    square = jnp.sum(jnp.where(lane == count, products, 0.0), axis=1, keepdims=True)
    index = iota((LANES, width), 1)
    which = iota((LANES, width), 0)
    many = jnp.broadcast_to(projection, (8, LANES))
    outer = dot(many, ones_where(index // count == which, jnp.float32), precision=HIGHEST)
    inner = dot(many, ones_where(index % count == which, jnp.float32), precision=HIGHEST)
    squares = (
        square
        - 2.0 * jnp.sum(projection * products, axis=1, keepdims=True)
        + jnp.sum(gram * outer[:1] * inner[:1], axis=1, keepdims=True)
    )
    new_norm = jnp.sqrt(squares / all_panels + 1e-06)
    remainder = image_ref[...]
    for k in range(count):
        remainder = remainder - projection[:, k : k + 1] * basis_ref[k, 0]
    next_ref[0] = remainder / new_norm
    column = jnp.where(lane == count, new_norm, projection)
    hessenberg_ref[...] = column[:, : count + 1]


def exchange(rows, axes):
    return lax.all_to_all(rows, axes, 0, 0)


def neighbour(value, step):
    count = lax.axis_size(CL)
    route = [(i, i + step) for i in range(count) if 0 <= i + step < count]
    return lax.ppermute(value, CL, route)


def f32(*shape):
    return jax.ShapeDtypeStruct(shape, jnp.float32)


def bf16(*shape):
    return jax.ShapeDtypeStruct(shape, jnp.bfloat16)


def on_device(
    basis,
    near_blocks,
    near_list,
    source_basis,
    target_basis,
    coupling,
    far_target,
    far_source,
    far_count,
):
    count, _, clusters, panels = basis.shape
    ranks = source_basis.shape[2]
    slots = coupling.shape[1]
    owners = lax.axis_size(CL)
    width = clusters * ranks
    packed = count * count + LANES

    last = pl.BlockSpec((1, 1, clusters, panels), lambda i: (count - 1, 0, 0, 0))
    sent = pl.pallas_call(
        expand_kernel,
        grid=(1,),
        in_specs=[last, pl.BlockSpec(source_basis.shape, lambda i: (0, 0, 0, 0))],
        out_specs=pl.BlockSpec((owners, width // LANES, LANES), lambda i: (0, 0, 0)),
        out_shape=bf16(owners, width // LANES, LANES),
        name="expand",
    )(basis, source_basis)
    expansions = exchange(sent, CL)
    current = pl.pallas_call(
        current_kernel,
        grid=(1,),
        in_specs=[last, pl.BlockSpec(memory_space=pl.ANY)],
        out_specs=pl.BlockSpec((clusters, panels), lambda i: (0, 0)),
        out_shape=bf16(clusters, panels),
        cost_estimate=pl.CostEstimate(flops=0, bytes_accessed=1 << 26, transcendentals=0),
        name="current",
    )(basis, sent)
    before = neighbour(current, 1)
    after = neighbour(current, -1)

    me = lax.axis_index(CL)
    targets = lax.dynamic_slice_in_dim(far_target, me * slots, slots, axis=1)
    sent = pl.pallas_call(
        lambda *refs: far_kernel(clusters, owners, *refs),
        in_specs=[SMEM, SMEM, SMEM, VMEM, VMEM],
        out_specs=VMEM,
        out_shape=f32(owners, 1, width),
        compiler_params=SMALL,
        name="far",
    )(far_source, targets, far_count, expansions, coupling)
    arrived = exchange(sent, CL)

    window = jnp.concatenate([before, current, after], axis=0)
    near = jnp.einsum(
        "tkij,tkj->ti", near_blocks[0], window[near_list[0]], preferred_element_type=jnp.float32
    )
    gram = pl.pallas_call(
        gram_kernel, in_specs=[VMEM], out_specs=VMEM, out_shape=f32(1, count * count), compiler_params=SMALL, name="gram"
    )(basis)
    image, sent = pl.pallas_call(
        lambda *refs: image_kernel(owners, *refs),
        in_specs=[VMEM] * 5,
        out_specs=[VMEM] * 2,
        out_shape=[f32(clusters, panels), f32(lax.axis_size(ROW), 1, packed)],
        compiler_params=SMALL,
        name="image",
    )(basis, target_basis, arrived, near, gram)
    sent = pl.pallas_call(
        total_kernel,
        in_specs=[VMEM],
        out_specs=VMEM,
        out_shape=f32(lax.axis_size(COLUMN), 1, packed),
        compiler_params=SMALL,
        name="total",
    )(exchange(sent, ROW))
    all_panels = float(owners * lax.axis_size("grp") * clusters * panels)
    next_vector, hessenberg = pl.pallas_call(
        lambda *refs: final_kernel(all_panels, *refs),
        in_specs=[VMEM] * 3,
        out_specs=[VMEM] * 2,
        out_shape=[f32(1, clusters, panels), f32(1, count + 1)],
        compiler_params=SMALL,
        name="final",
    )(basis, image, exchange(sent, COLUMN))
    return (next_vector, hessenberg.reshape(count + 1))


def solution(mesh):
    torus = Mesh(mesh.devices.reshape(8, 8, 2, mesh.shape["grp"]), (*CL, "grp"))
    in_specs = (
        P(None, "grp", CL, None),
        P("grp", CL, None, None, None),
        P("grp", CL, None),
        P("grp", CL, None, None),
        P("grp", CL, None, None),
        P("grp", CL, None),
        P("grp", None),
        P("grp", CL),
        P("grp", CL),
    )
    return jax.shard_map(
        on_device,
        mesh=torus,
        in_specs=in_specs,
        out_specs=(P("grp", CL, None), P()),
        check_vma=False,
    )
```

```python
import jax
import jax.numpy as jnp
from jax import lax
from jax.experimental import pallas as pl
from jax.experimental.pallas import tpu as pltpu
from jax.sharding import Mesh
from jax.sharding import PartitionSpec as P

CL = ("z", "x", "core")
ROW = ("x", "core")
COLUMN = ("z", "grp")
HIGHEST = lax.Precision.HIGHEST
LANES = 128
SHARERS = 8
FIRST, LAST = -2, 3

SMALL = pltpu.CompilerParams(vmem_limit_bytes=4 * 1024 * 1024)
VMEM = pl.BlockSpec(memory_space=pltpu.VMEM)
ANY = pl.BlockSpec(memory_space=pl.ANY)
HBM = pl.BlockSpec(memory_space=pltpu.HBM)
SMEM = pl.BlockSpec(memory_space=pltpu.SMEM)


def iota(shape, dim):
    return lax.broadcasted_iota(jnp.int32, shape, dim)


def dot(a, b, contract=((1,), (0,)), precision=None):
    return lax.dot_general(
        a, b, (contract, ((), ())), precision=precision, preferred_element_type=jnp.float32
    )


def ones_where(mask, dtype):
    return jnp.where(mask, 1.0, 0.0).astype(dtype)


def position():
    return lax.axis_index("z") * 16 + lax.axis_index("x") * 2 + lax.axis_index("core")


def relay_kernel(tile_ref, after_ref, relayed_ref):
    relayed_ref[...] = tile_ref[...]


def expand_kernel(
    basis_ref,
    source_ref,
    target_ref,
    sent_ref,
    current_ref,
    window_ref,
    tile_ref,
    matrix_ref,
    semaphores,
):
    count, _, clusters, panels = basis_ref.shape
    ranks = source_ref.shape[2]
    width = clusters * ranks
    first = pl.multiple_of(position() // SHARERS * LANES, LANES)
    copies = [
        pltpu.make_async_copy(basis_ref.at[count - 1, 0], tile_ref, semaphores.at[0]),
        pltpu.make_async_copy(source_ref.at[0], matrix_ref, semaphores.at[1]),
        pltpu.make_async_copy(target_ref.at[:, pl.ds(first, LANES)], window_ref, semaphores.at[2]),
    ]
    for copy in copies:
        copy.start()
    copies[0].wait()
    current = tile_ref[...].astype(jnp.bfloat16)
    current_ref[...] = current
    copies[1].wait()
    every = dot(current, matrix_ref[...].reshape(width, panels), ((1,), (1,)))
    own = iota((clusters, width), 1) // ranks == iota((clusters, width), 0)
    row = jnp.sum(jnp.where(own, every, 0.0), axis=0, keepdims=True)
    pieces = [row[:, i : i + LANES] for i in range(0, width, LANES)]
    tile = jnp.concatenate(pieces, axis=0).astype(jnp.bfloat16)
    sent_ref[...] = jnp.broadcast_to(tile[None], sent_ref.shape)
    copies[2].wait()


def far_kernel(
    clusters, owners, source_ref, target_ref, count_ref, expansion_ref, coupling_ref, sent_ref
):
    slots = coupling_ref.shape[1]
    width = sent_ref.shape[2]
    ranks = width // clusters
    groups = LANES // ranks
    parts = ranks // groups
    me = position()
    lane_cluster = iota((1, width), 1) // ranks
    tile = expansion_ref.shape[1:]
    place = iota(tile, 0) * groups + iota(tile, 1) // ranks
    picked, targets = [], []
    for b in range(slots):
        source = source_ref[0, b]
        rows = expansion_ref[source // clusters].astype(jnp.float32)
        rows = jnp.where(place == source % clusters, rows, 0.0)
        picked.append(jnp.sum(rows, axis=0, keepdims=True))
        target = jnp.where(b < count_ref[0, 0], target_ref[0, lax.rem(me, SHARERS) * slots + b], -1)
        targets.append(jnp.full((1, width), target, jnp.int32))
    picked = jnp.concatenate(picked, axis=0).astype(jnp.bfloat16)
    targets = jnp.concatenate(targets, axis=0)
    spread = iota((LANES, LANES), 0) % ranks == iota((LANES, LANES), 1) % ranks
    vector = dot(picked, ones_where(spread, jnp.bfloat16))
    coupling = coupling_ref[0].astype(jnp.float32)
    high, low = [], []
    for q in range(parts):
        product = coupling[:, q * LANES : (q + 1) * LANES] * vector
        top = product.astype(jnp.bfloat16)
        high.append(top)
        low.append((product - top.astype(jnp.float32)).astype(jnp.bfloat16))
    gather = iota((LANES, width), 0) // ranks == iota((LANES, width), 1) % groups
    sums = dot(jnp.concatenate(high + low, axis=0), ones_where(gather, jnp.bfloat16))
    part = (iota((slots, width), 1) % ranks) // groups
    term = jnp.zeros((slots, width), jnp.float32)
    for q in range(parts):
        value = sums[q * slots : (q + 1) * slots] + sums[(parts + q) * slots : (parts + q + 1) * slots]
        term = jnp.where(part == q, value, term)
    sent_ref[...] = jnp.zeros_like(sent_ref)

    def send(owner):
        mine = targets == owner * clusters + lane_cluster
        sent_ref[owner] = jnp.sum(jnp.where(mine, term, 0.0), axis=0, keepdims=True)

    for step in range(FIRST, LAST + 1):
        owner = me + step

        @pl.when(jnp.logical_and(owner >= 0, owner < owners))
        def _():
            send(owner)

    send(lax.rem(me + owners // 2, owners))


def gram_kernel(basis_ref, after_ref, gram_ref):
    count, _, clusters, _ = basis_ref.shape
    gram = jnp.zeros((count, count), jnp.float32)
    for c in range(clusters):
        rows = basis_ref[:, 0, c, :]
        gram = gram + dot(rows, rows, ((1,), (1,)), HIGHEST)
    width = count * count
    tile = iota((count, width), 1) % count == iota((count, width), 0)
    rows = dot(gram, ones_where(tile, jnp.float32), precision=HIGHEST)
    own = iota((count, width), 1) // count == iota((count, width), 0)
    gram_ref[...] = jnp.sum(jnp.where(own, rows, 0.0), axis=0, keepdims=True)


def image_kernel(owners, basis_ref, target_ref, arrived_ref, near_ref, gram_ref, image_ref, sent_ref):
    count = basis_ref.shape[0]
    clusters, panels = near_ref.shape
    ranks = target_ref.shape[2]
    width = clusters * ranks
    me = position()
    coupled = arrived_ref[lax.rem(me + owners // 2, owners)]
    for step in range(-LAST, -FIRST + 1):
        owner = me + step
        inside = jnp.logical_and(owner >= 0, owner < owners)
        value = arrived_ref[jnp.clip(owner, 0, owners - 1)]
        coupled = coupled + jnp.where(inside, value, 0.0)
    own = iota((clusters, width), 1) // ranks == iota((clusters, width), 0)
    spread = jnp.where(own, coupled, 0.0).astype(jnp.bfloat16)
    far = dot(spread, target_ref[0].reshape(width, panels))
    image = 0.5 * basis_ref[count - 1, 0] + near_ref[...] + far
    image_ref[...] = image
    rows = [jnp.sum(basis_ref[k, 0] * image, axis=0, keepdims=True) for k in range(count)]
    rows.append(jnp.sum(image * image, axis=0, keepdims=True))
    rows.append(jnp.zeros((LANES - count - 1, panels), jnp.float32))
    products = dot(
        jnp.ones((8, panels), jnp.float32), jnp.concatenate(rows, axis=0), ((1,), (1,)), HIGHEST
    )
    row = jnp.concatenate([gram_ref[...], products[:1]], axis=1)
    sent_ref[...] = jnp.broadcast_to(row[None], sent_ref.shape)


def total_kernel(arrived_ref, sent_ref):
    sent_ref[...] = jnp.broadcast_to(
        jnp.sum(arrived_ref[...], axis=0, keepdims=True), sent_ref.shape
    )


def final_kernel(all_panels, basis_ref, image_ref, arrived_ref, next_ref, hessenberg_ref):
    count = basis_ref.shape[0]
    width = count * count
    total = jnp.sum(arrived_ref[...], axis=0)
    gram = total[:, :width]
    products = total[:, width:]
    lane = iota((1, LANES), 1)
    projection = jnp.where(lane < count, products / all_panels, 0.0)
    square = jnp.sum(jnp.where(lane == count, products, 0.0), axis=1, keepdims=True)
    index = iota((LANES, width), 1)
    which = iota((LANES, width), 0)
    many = jnp.broadcast_to(projection, (8, LANES))
    outer = dot(many, ones_where(index // count == which, jnp.float32), precision=HIGHEST)
    inner = dot(many, ones_where(index % count == which, jnp.float32), precision=HIGHEST)
    squares = (
        square
        - 2.0 * jnp.sum(projection * products, axis=1, keepdims=True)
        + jnp.sum(gram * outer[:1] * inner[:1], axis=1, keepdims=True)
    )
    new_norm = jnp.sqrt(squares / all_panels + 1e-06)
    remainder = image_ref[...]
    for k in range(count):
        remainder = remainder - projection[:, k : k + 1] * basis_ref[k, 0]
    next_ref[0] = remainder / new_norm
    column = jnp.where(lane == count, new_norm, projection)
    hessenberg_ref[...] = column[:, : count + 1]


def exchange(rows, axes):
    return lax.all_to_all(rows, axes, 0, 0)


def neighbour(value, step):
    count = lax.axis_size(CL)
    route = [(i, i + step) for i in range(count) if 0 <= i + step < count]
    return lax.ppermute(value, CL, route)


def f32(*shape):
    return jax.ShapeDtypeStruct(shape, jnp.float32)


def bf16(*shape):
    return jax.ShapeDtypeStruct(shape, jnp.bfloat16)


def on_device(
    basis,
    near_blocks,
    near_list,
    source_basis,
    target_basis,
    coupling,
    far_target,
    far_source,
    far_count,
):
    count, _, clusters, panels = basis.shape
    ranks = source_basis.shape[2]
    slots = coupling.shape[1]
    owners = lax.axis_size(CL)
    width = clusters * ranks
    packed = count * count + LANES

    sent, current, targets = pl.pallas_call(
        expand_kernel,
        in_specs=[HBM, HBM, HBM],
        out_specs=[VMEM, VMEM, SMEM],
        out_shape=[
            bf16(owners, width // LANES, LANES),
            bf16(clusters, panels),
            jax.ShapeDtypeStruct((1, LANES), jnp.int32),
        ],
        scratch_shapes=[
            pltpu.VMEM((clusters, panels), jnp.float32),
            pltpu.VMEM((clusters, ranks, panels), jnp.bfloat16),
            pltpu.SemaphoreType.DMA((3,)),
        ],
        name="expand",
    )(basis, source_basis, far_target)
    expansions = exchange(sent, CL)
    current = pl.pallas_call(
        relay_kernel,
        in_specs=[VMEM, ANY],
        out_specs=VMEM,
        out_shape=bf16(clusters, panels),
        compiler_params=SMALL,
        cost_estimate=pl.CostEstimate(flops=0, bytes_accessed=1 << 26, transcendentals=0),
        name="relay",
    )(current, sent)
    before = neighbour(current, 1)
    after = neighbour(current, -1)

    sent = pl.pallas_call(
        lambda *refs: far_kernel(clusters, owners, *refs),
        in_specs=[SMEM, SMEM, SMEM, VMEM, VMEM],
        out_specs=VMEM,
        out_shape=f32(owners, 1, width),
        compiler_params=SMALL,
        name="far",
    )(far_source, targets, far_count, expansions, coupling)
    arrived = exchange(sent, CL)

    window = jnp.concatenate([before, current, after], axis=0)
    near = jnp.einsum(
        "tkij,tkj->ti", near_blocks[0], window[near_list[0]], preferred_element_type=jnp.float32
    )
    gram = pl.pallas_call(
        gram_kernel,
        in_specs=[VMEM, ANY],
        out_specs=VMEM,
        out_shape=f32(1, count * count),
        compiler_params=SMALL,
        name="gram",
    )(basis, after)
    image, sent = pl.pallas_call(
        lambda *refs: image_kernel(owners, *refs),
        in_specs=[VMEM] * 5,
        out_specs=[VMEM] * 2,
        out_shape=[f32(clusters, panels), f32(lax.axis_size(ROW), 1, packed)],
        compiler_params=SMALL,
        name="image",
    )(basis, target_basis, arrived, near, gram)
    sent = pl.pallas_call(
        total_kernel,
        in_specs=[VMEM],
        out_specs=VMEM,
        out_shape=f32(lax.axis_size(COLUMN), 1, packed),
        compiler_params=SMALL,
        name="total",
    )(exchange(sent, ROW))
    all_panels = float(owners * lax.axis_size("grp") * clusters * panels)
    next_vector, hessenberg = pl.pallas_call(
        lambda *refs: final_kernel(all_panels, *refs),
        in_specs=[VMEM] * 3,
        out_specs=[VMEM] * 2,
        out_shape=[f32(1, clusters, panels), f32(1, count + 1)],
        compiler_params=SMALL,
        name="final",
    )(basis, image, exchange(sent, COLUMN))
    return (next_vector, hessenberg.reshape(count + 1))


def solution(mesh):
    torus = Mesh(mesh.devices.reshape(8, 8, 2, mesh.shape["grp"]), (*CL, "grp"))
    in_specs = (
        P(None, "grp", CL, None),
        P("grp", CL, None, None, None),
        P("grp", CL, None),
        P("grp", CL, None, None),
        P("grp", CL, None, None),
        P("grp", CL, None),
        P("grp", None),
        P("grp", CL),
        P("grp", CL),
    )
    return jax.shard_map(
        on_device,
        mesh=torus,
        in_specs=in_specs,
        out_specs=(P("grp", CL, None), P()),
        check_vma=False,
    )
```

```python
import jax
import jax.numpy as jnp
from jax import lax
from jax.experimental import pallas as pl
from jax.experimental.pallas import tpu as pltpu
from jax.sharding import Mesh
from jax.sharding import PartitionSpec as P

CL = ("z", "x", "core")
ROW = ("x", "core")
COLUMN = ("z", "grp")
HIGHEST = lax.Precision.HIGHEST
LANES = 128
SHARERS = 8
FIRST, LAST = -2, 3

SMALL = pltpu.CompilerParams(vmem_limit_bytes=4 * 1024 * 1024)
VMEM = pl.BlockSpec(memory_space=pltpu.VMEM)
ANY = pl.BlockSpec(memory_space=pl.ANY)
HBM = pl.BlockSpec(memory_space=pltpu.HBM)
SMEM = pl.BlockSpec(memory_space=pltpu.SMEM)


def iota(shape, dim):
    return lax.broadcasted_iota(jnp.int32, shape, dim)


def dot(a, b, contract=((1,), (0,)), precision=None):
    return lax.dot_general(
        a, b, (contract, ((), ())), precision=precision, preferred_element_type=jnp.float32
    )


def ones_where(mask, dtype):
    return jnp.where(mask, 1.0, 0.0).astype(dtype)


def position():
    return lax.axis_index("z") * 16 + lax.axis_index("x") * 2 + lax.axis_index("core")


def relay_kernel(tile_ref, after_ref, relayed_ref):
    relayed_ref[...] = tile_ref[...]


def expand_kernel(
    basis_ref,
    source_ref,
    target_ref,
    sent_ref,
    current_ref,
    window_ref,
    tile_ref,
    matrix_ref,
    semaphores,
):
    count, _, clusters, panels = basis_ref.shape
    ranks = source_ref.shape[2]
    width = clusters * ranks
    first = pl.multiple_of(position() // SHARERS * LANES, LANES)
    copies = [
        pltpu.make_async_copy(basis_ref.at[count - 1, 0], tile_ref, semaphores.at[0]),
        pltpu.make_async_copy(source_ref.at[0], matrix_ref, semaphores.at[1]),
        pltpu.make_async_copy(target_ref.at[:, pl.ds(first, LANES)], window_ref, semaphores.at[2]),
    ]
    for copy in copies:
        copy.start()
    copies[0].wait()
    current = tile_ref[...].astype(jnp.bfloat16)
    current_ref[...] = current
    copies[1].wait()
    every = dot(current, matrix_ref[...].reshape(width, panels), ((1,), (1,)))
    own = iota((clusters, width), 1) // ranks == iota((clusters, width), 0)
    row = jnp.sum(jnp.where(own, every, 0.0), axis=0, keepdims=True)
    pieces = [row[:, i : i + LANES] for i in range(0, width, LANES)]
    tile = jnp.concatenate(pieces, axis=0).astype(jnp.bfloat16)
    sent_ref[...] = jnp.broadcast_to(tile[None], sent_ref.shape)
    copies[2].wait()


def far_kernel(
    clusters,
    owners,
    source_ref,
    target_ref,
    count_ref,
    expansion_ref,
    coupling_ref,
    current_ref,
    sent_ref,
    held_ref,
):
    held_ref[...] = current_ref[...]
    slots = coupling_ref.shape[1]
    width = expansion_ref.shape[1] * LANES
    ranks = width // clusters
    groups = LANES // ranks
    parts = ranks // groups
    me = position()
    lane_cluster = iota((1, width), 1) // ranks
    tile = expansion_ref.shape[1:]
    place = iota(tile, 0) * groups + iota(tile, 1) // ranks
    picked, targets = [], []
    for b in range(slots):
        source = source_ref[0, b]
        rows = expansion_ref[source // clusters].astype(jnp.float32)
        rows = jnp.where(place == source % clusters, rows, 0.0)
        picked.append(jnp.sum(rows, axis=0, keepdims=True))
        target = jnp.where(b < count_ref[0, 0], target_ref[0, lax.rem(me, SHARERS) * slots + b], -1)
        targets.append(jnp.full((1, width), target, jnp.int32))
    picked = jnp.concatenate(picked, axis=0).astype(jnp.bfloat16)
    targets = jnp.concatenate(targets, axis=0)
    spread = iota((LANES, LANES), 0) % ranks == iota((LANES, LANES), 1) % ranks
    vector = dot(picked, ones_where(spread, jnp.bfloat16))
    coupling = coupling_ref[0].astype(jnp.float32)
    high, low = [], []
    for q in range(parts):
        product = coupling[:, q * LANES : (q + 1) * LANES] * vector
        top = product.astype(jnp.bfloat16)
        high.append(top)
        low.append((product - top.astype(jnp.float32)).astype(jnp.bfloat16))
    gather = iota((LANES, width), 0) // ranks == iota((LANES, width), 1) % groups
    sums = dot(jnp.concatenate(high + low, axis=0), ones_where(gather, jnp.bfloat16))
    part = (iota((slots, width), 1) % ranks) // groups
    term = jnp.zeros((slots, width), jnp.float32)
    for q in range(parts):
        value = sums[q * slots : (q + 1) * slots] + sums[(parts + q) * slots : (parts + q + 1) * slots]
        term = jnp.where(part == q, value, term)
    sent_ref[...] = jnp.zeros_like(sent_ref)

    def send(owner):
        mine = targets == owner * clusters + lane_cluster
        row = jnp.sum(jnp.where(mine, term, 0.0), axis=0, keepdims=True)
        pieces = [row[:, i : i + LANES] for i in range(0, width, LANES)]
        sent_ref[owner] = jnp.concatenate(pieces, axis=0).astype(jnp.bfloat16)

    for step in range(FIRST, LAST + 1):
        owner = me + step

        @pl.when(jnp.logical_and(owner >= 0, owner < owners))
        def _():
            send(owner)

    send(lax.rem(me + owners // 2, owners))


def kept(count):
    return count * (count // 2 + 1)


def gram_kernel(basis_ref, after_ref, gram_ref):
    count, _, clusters, _ = basis_ref.shape
    gram = jnp.zeros((count, count), jnp.float32)
    for c in range(clusters):
        rows = basis_ref[:, 0, c, :]
        gram = gram + dot(rows, rows, ((1,), (1,)), HIGHEST)
    lane = iota((count, gram_ref.shape[1]), 1)
    row = iota((count, gram_ref.shape[1]), 0)
    pick = jnp.logical_and((lane + lane // count) % count == row, lane < kept(count))
    rows = dot(gram, ones_where(pick, jnp.float32), precision=HIGHEST)
    gram_ref[...] = jnp.sum(jnp.where(lane % count == row, rows, 0.0), axis=0, keepdims=True)


def image_kernel(owners, basis_ref, target_ref, arrived_ref, near_ref, gram_ref, image_ref, sent_ref):
    count = basis_ref.shape[0]
    clusters, panels = near_ref.shape
    ranks = target_ref.shape[2]
    width = clusters * ranks
    me = position()
    coupled = arrived_ref[lax.rem(me + owners // 2, owners)].astype(jnp.float32)
    for step in range(-LAST, -FIRST + 1):
        owner = me + step
        inside = jnp.logical_and(owner >= 0, owner < owners)
        value = arrived_ref[jnp.clip(owner, 0, owners - 1)].astype(jnp.float32)
        coupled = coupled + jnp.where(inside, value, 0.0)
    coupled = jnp.concatenate([coupled[i : i + 1] for i in range(coupled.shape[0])], axis=1)
    own = iota((clusters, width), 1) // ranks == iota((clusters, width), 0)
    spread = jnp.where(own, coupled, 0.0).astype(jnp.bfloat16)
    far = dot(spread, target_ref[0].reshape(width, panels))
    image = 0.5 * basis_ref[count - 1, 0] + near_ref[...] + far
    image_ref[...] = image
    first = kept(count) % LANES
    rows = [jnp.zeros((first, panels), jnp.float32)]
    rows += [jnp.sum(basis_ref[k, 0] * image, axis=0, keepdims=True) for k in range(count)]
    rows.append(jnp.sum(image * image, axis=0, keepdims=True))
    rows.append(jnp.zeros((LANES - first - count - 1, panels), jnp.float32))
    products = dot(
        jnp.ones((8, panels), jnp.float32), jnp.concatenate(rows, axis=0), ((1,), (1,)), HIGHEST
    )
    gram = gram_ref[...]
    row = jnp.concatenate([gram[:, :LANES], gram[:, LANES:] + products[:1]], axis=1)
    sent_ref[...] = jnp.broadcast_to(row[None], sent_ref.shape)


def total_kernel(arrived_ref, sent_ref):
    sent_ref[...] = jnp.broadcast_to(
        jnp.sum(arrived_ref[...], axis=0, keepdims=True), sent_ref.shape
    )


def final_kernel(all_panels, basis_ref, image_ref, arrived_ref, next_ref, hessenberg_ref):
    count = basis_ref.shape[0]
    first = kept(count) % LANES
    total = jnp.sum(arrived_ref[...], axis=0)
    products = total[:, LANES:]
    lane = iota((1, LANES), 1)
    inside = jnp.logical_and(lane >= first, lane < first + count)
    projection = jnp.where(inside, products / all_panels, 0.0)
    square = jnp.sum(jnp.where(lane == first + count, products, 0.0), axis=1, keepdims=True)
    index = iota((LANES, total.shape[1]), 1)
    which = iota((LANES, total.shape[1]), 0) - first
    many = jnp.broadcast_to(projection, (8, LANES))
    outer = dot(many, ones_where(index % count == which, jnp.float32), precision=HIGHEST)
    shifted = (index + index // count) % count == which
    inner = dot(many, ones_where(shifted, jnp.float32), precision=HIGHEST)
    diagonal = iota(total.shape, 1) // count
    once = jnp.logical_or(diagonal == 0, diagonal == count // 2)
    gram = jnp.where(diagonal <= count // 2, total * jnp.where(once, 1.0, 2.0), 0.0)
    squares = (
        square
        - 2.0 * jnp.sum(projection * products, axis=1, keepdims=True)
        + jnp.sum(gram * outer[:1] * inner[:1], axis=1, keepdims=True)
    )
    new_norm = jnp.sqrt(squares / all_panels + 1e-06)
    remainder = image_ref[...]
    for k in range(count):
        remainder = remainder - projection[:, first + k : first + k + 1] * basis_ref[k, 0]
    next_ref[0] = remainder / new_norm
    column = jnp.where(lane == first + count, new_norm, projection)
    hessenberg_ref[...] = column[:, first : first + count + 1]


def exchange(rows, axes):
    return lax.all_to_all(rows, axes, 0, 0)


def neighbour(value, step):
    count = lax.axis_size(CL)
    route = [(i, i + step) for i in range(count) if 0 <= i + step < count]
    return lax.ppermute(value, CL, route)


def f32(*shape):
    return jax.ShapeDtypeStruct(shape, jnp.float32)


def bf16(*shape):
    return jax.ShapeDtypeStruct(shape, jnp.bfloat16)


def on_device(
    basis,
    near_blocks,
    near_list,
    source_basis,
    target_basis,
    coupling,
    far_target,
    far_source,
    far_count,
):
    count, _, clusters, panels = basis.shape
    ranks = source_basis.shape[2]
    slots = coupling.shape[1]
    owners = lax.axis_size(CL)
    width = clusters * ranks
    packed = 2 * LANES

    sent, current, targets = pl.pallas_call(
        expand_kernel,
        in_specs=[HBM, HBM, HBM],
        out_specs=[VMEM, VMEM, SMEM],
        out_shape=[
            bf16(owners, width // LANES, LANES),
            bf16(clusters, panels),
            jax.ShapeDtypeStruct((1, LANES), jnp.int32),
        ],
        scratch_shapes=[
            pltpu.VMEM((clusters, panels), jnp.float32),
            pltpu.VMEM((clusters, ranks, panels), jnp.bfloat16),
            pltpu.SemaphoreType.DMA((3,)),
        ],
        name="expand",
    )(basis, source_basis, far_target)
    expansions = exchange(sent, CL)
    current = pl.pallas_call(
        relay_kernel,
        in_specs=[VMEM, ANY],
        out_specs=VMEM,
        out_shape=bf16(clusters, panels),
        compiler_params=SMALL,
        cost_estimate=pl.CostEstimate(flops=0, bytes_accessed=1 << 26, transcendentals=0),
        name="relay",
    )(current, sent)
    before = neighbour(current, 1)
    after = neighbour(current, -1)

    sent, held = pl.pallas_call(
        lambda *refs: far_kernel(clusters, owners, *refs),
        in_specs=[SMEM, SMEM, SMEM, VMEM, VMEM, VMEM],
        out_specs=[VMEM, VMEM],
        out_shape=[bf16(owners, width // LANES, LANES), bf16(clusters, panels)],
        compiler_params=SMALL,
        name="far",
    )(far_source, targets, far_count, expansions, coupling, current)
    arrived = exchange(sent, CL)

    window = jnp.concatenate([before, held, after], axis=0)
    near = jnp.einsum(
        "tkij,tkj->ti", near_blocks[0], window[near_list[0]], preferred_element_type=jnp.float32
    )
    gram = pl.pallas_call(
        gram_kernel,
        in_specs=[VMEM, ANY],
        out_specs=VMEM,
        out_shape=f32(1, packed),
        compiler_params=SMALL,
        name="gram",
    )(basis, held)
    image, sent = pl.pallas_call(
        lambda *refs: image_kernel(owners, *refs),
        in_specs=[VMEM] * 5,
        out_specs=[VMEM] * 2,
        out_shape=[f32(clusters, panels), f32(lax.axis_size(ROW), 1, packed)],
        compiler_params=SMALL,
        name="image",
    )(basis, target_basis, arrived, near, gram)
    sent = pl.pallas_call(
        total_kernel,
        in_specs=[VMEM],
        out_specs=VMEM,
        out_shape=f32(lax.axis_size(COLUMN), 1, packed),
        compiler_params=SMALL,
        name="total",
    )(exchange(sent, ROW))
    all_panels = float(owners * lax.axis_size("grp") * clusters * panels)
    next_vector, hessenberg = pl.pallas_call(
        lambda *refs: final_kernel(all_panels, *refs),
        in_specs=[VMEM] * 3,
        out_specs=[VMEM] * 2,
        out_shape=[f32(1, clusters, panels), f32(1, count + 1)],
        compiler_params=SMALL,
        name="final",
    )(basis, image, exchange(sent, COLUMN))
    return (next_vector, hessenberg.reshape(count + 1))


def solution(mesh):
    torus = Mesh(mesh.devices.reshape(8, 8, 2, mesh.shape["grp"]), (*CL, "grp"))
    in_specs = (
        P(None, "grp", CL, None),
        P("grp", CL, None, None, None),
        P("grp", CL, None),
        P("grp", CL, None, None),
        P("grp", CL, None, None),
        P("grp", CL, None),
        P("grp", None),
        P("grp", CL),
        P("grp", CL),
    )
    return jax.shard_map(
        on_device,
        mesh=torus,
        in_specs=in_specs,
        out_specs=(P("grp", CL, None), P()),
        check_vma=False,
    )
```

```python
import jax
import jax.numpy as jnp
from jax import lax
from jax.experimental import pallas as pl
from jax.experimental.pallas import tpu as pltpu
from jax.sharding import Mesh
from jax.sharding import PartitionSpec as P

CL = ("z", "x", "core")
ROW = ("x", "core")
COLUMN = ("z", "grp")
HIGHEST = lax.Precision.HIGHEST
LANES = 128
SHARERS = 8
FIRST, LAST = -2, 3

SMALL = pltpu.CompilerParams(vmem_limit_bytes=4 * 1024 * 1024)
VMEM = pl.BlockSpec(memory_space=pltpu.VMEM)
ANY = pl.BlockSpec(memory_space=pl.ANY)
HBM = pl.BlockSpec(memory_space=pltpu.HBM)
SMEM = pl.BlockSpec(memory_space=pltpu.SMEM)


def iota(shape, dim):
    return lax.broadcasted_iota(jnp.int32, shape, dim)


def dot(a, b, contract=((1,), (0,)), precision=None):
    return lax.dot_general(
        a, b, (contract, ((), ())), precision=precision, preferred_element_type=jnp.float32
    )


def ones_where(mask, dtype):
    return jnp.where(mask, 1.0, 0.0).astype(dtype)


def position():
    return lax.axis_index("z") * 16 + lax.axis_index("x") * 2 + lax.axis_index("core")


def relay_kernel(tile_ref, targets_ref, sources_ref, after_ref, *relayed):
    for given, passed in zip((tile_ref, targets_ref, sources_ref), relayed):
        passed[...] = given[...]


def expand_kernel(
    basis_ref,
    source_ref,
    target_ref,
    sent_ref,
    current_ref,
    window_ref,
    tile_ref,
    matrix_ref,
    semaphores,
):
    count, _, clusters, panels = basis_ref.shape
    ranks = source_ref.shape[2]
    width = clusters * ranks
    first = pl.multiple_of(position() // SHARERS * LANES, LANES)
    copies = [
        pltpu.make_async_copy(basis_ref.at[count - 1, 0], tile_ref, semaphores.at[0]),
        pltpu.make_async_copy(source_ref.at[0], matrix_ref, semaphores.at[1]),
        pltpu.make_async_copy(target_ref.at[:, pl.ds(first, LANES)], window_ref, semaphores.at[2]),
    ]
    for copy in copies:
        copy.start()
    copies[0].wait()
    current = tile_ref[...].astype(jnp.bfloat16)
    current_ref[...] = current
    copies[1].wait()
    every = dot(current, matrix_ref[...].reshape(width, panels), ((1,), (1,)))
    own = iota((clusters, width), 1) // ranks == iota((clusters, width), 0)
    row = jnp.sum(jnp.where(own, every, 0.0), axis=0, keepdims=True)
    pieces = [row[:, i : i + LANES] for i in range(0, width, LANES)]
    tile = jnp.concatenate(pieces, axis=0).astype(jnp.bfloat16)
    sent_ref[...] = jnp.broadcast_to(tile[None], sent_ref.shape)
    copies[2].wait()


def far_kernel(
    clusters,
    owners,
    source_ref,
    target_ref,
    count_ref,
    expansion_ref,
    coupling_ref,
    current_ref,
    sent_ref,
    held_ref,
):
    held_ref[...] = current_ref[...]
    slots = coupling_ref.shape[1]
    width = expansion_ref.shape[1] * LANES
    ranks = width // clusters
    groups = LANES // ranks
    parts = ranks // groups
    me = position()
    lane_cluster = iota((1, width), 1) // ranks
    tile = expansion_ref.shape[1:]
    place = iota(tile, 0) * groups + iota(tile, 1) // ranks
    picked, targets = [], []
    for b in range(slots):
        source = source_ref[0, b]
        rows = expansion_ref[source // clusters].astype(jnp.float32)
        rows = jnp.where(place == source % clusters, rows, 0.0)
        picked.append(jnp.sum(rows, axis=0, keepdims=True))
        target = jnp.where(b < count_ref[0, 0], target_ref[0, lax.rem(me, SHARERS) * slots + b], -1)
        targets.append(jnp.full((1, width), target, jnp.int32))
    picked = jnp.concatenate(picked, axis=0).astype(jnp.bfloat16)
    targets = jnp.concatenate(targets, axis=0)
    spread = iota((LANES, LANES), 0) % ranks == iota((LANES, LANES), 1) % ranks
    vector = dot(picked, ones_where(spread, jnp.bfloat16))
    coupling = coupling_ref[0].astype(jnp.float32)
    high, low = [], []
    for q in range(parts):
        product = coupling[:, q * LANES : (q + 1) * LANES] * vector
        top = product.astype(jnp.bfloat16)
        high.append(top)
        low.append((product - top.astype(jnp.float32)).astype(jnp.bfloat16))
    gather = iota((LANES, width), 0) // ranks == iota((LANES, width), 1) % groups
    sums = dot(jnp.concatenate(high + low, axis=0), ones_where(gather, jnp.bfloat16))
    part = (iota((slots, width), 1) % ranks) // groups
    term = jnp.zeros((slots, width), jnp.float32)
    for q in range(parts):
        value = sums[q * slots : (q + 1) * slots] + sums[(parts + q) * slots : (parts + q + 1) * slots]
        term = jnp.where(part == q, value, term)
    sent_ref[...] = jnp.zeros_like(sent_ref)

    def send(owner):
        mine = targets == owner * clusters + lane_cluster
        row = jnp.sum(jnp.where(mine, term, 0.0), axis=0, keepdims=True)
        pieces = [row[:, i : i + LANES] for i in range(0, width, LANES)]
        sent_ref[owner] = jnp.concatenate(pieces, axis=0).astype(jnp.bfloat16)

    for step in range(FIRST, LAST + 1):
        owner = me + step

        @pl.when(jnp.logical_and(owner >= 0, owner < owners))
        def _():
            send(owner)

    send(lax.rem(me + owners // 2, owners))


def kept(count):
    return count * (count // 2 + 1)


def gram_kernel(basis_ref, after_ref, gram_ref):
    count, _, clusters, _ = basis_ref.shape
    gram = jnp.zeros((count, count), jnp.float32)
    for c in range(clusters):
        rows = basis_ref[:, 0, c, :]
        gram = gram + dot(rows, rows, ((1,), (1,)), HIGHEST)
    lane = iota((count, gram_ref.shape[1]), 1)
    row = iota((count, gram_ref.shape[1]), 0)
    pick = jnp.logical_and((lane + lane // count) % count == row, lane < kept(count))
    rows = dot(gram, ones_where(pick, jnp.float32), precision=HIGHEST)
    gram_ref[...] = jnp.sum(jnp.where(lane % count == row, rows, 0.0), axis=0, keepdims=True)


def image_kernel(owners, basis_ref, target_ref, arrived_ref, near_ref, gram_ref, image_ref, sent_ref):
    count = basis_ref.shape[0]
    clusters, panels = near_ref.shape
    ranks = target_ref.shape[2]
    width = clusters * ranks
    me = position()
    coupled = arrived_ref[lax.rem(me + owners // 2, owners)].astype(jnp.float32)
    for step in range(-LAST, -FIRST + 1):
        owner = me + step
        inside = jnp.logical_and(owner >= 0, owner < owners)
        value = arrived_ref[jnp.clip(owner, 0, owners - 1)].astype(jnp.float32)
        coupled = coupled + jnp.where(inside, value, 0.0)
    coupled = jnp.concatenate([coupled[i : i + 1] for i in range(coupled.shape[0])], axis=1)
    own = iota((clusters, width), 1) // ranks == iota((clusters, width), 0)
    spread = jnp.where(own, coupled, 0.0).astype(jnp.bfloat16)
    far = dot(spread, target_ref[0].reshape(width, panels))
    image = 0.5 * basis_ref[count - 1, 0] + near_ref[...] + far
    image_ref[...] = image
    first = kept(count) % LANES
    rows = [jnp.zeros((first, panels), jnp.float32)]
    rows += [jnp.sum(basis_ref[k, 0] * image, axis=0, keepdims=True) for k in range(count)]
    rows.append(jnp.sum(image * image, axis=0, keepdims=True))
    rows.append(jnp.zeros((LANES - first - count - 1, panels), jnp.float32))
    products = dot(
        jnp.ones((8, panels), jnp.float32), jnp.concatenate(rows, axis=0), ((1,), (1,)), HIGHEST
    )
    gram = gram_ref[...]
    row = jnp.concatenate([gram[:, :LANES], gram[:, LANES:] + products[:1]], axis=1)
    sent_ref[...] = jnp.broadcast_to(row[None], sent_ref.shape)


def total_kernel(arrived_ref, sent_ref):
    sent_ref[...] = jnp.broadcast_to(
        jnp.sum(arrived_ref[...], axis=0, keepdims=True), sent_ref.shape
    )


def final_kernel(all_panels, basis_ref, image_ref, arrived_ref, next_ref, hessenberg_ref):
    count = basis_ref.shape[0]
    first = kept(count) % LANES
    total = jnp.sum(arrived_ref[...], axis=0)
    products = total[:, LANES:]
    lane = iota((1, LANES), 1)
    inside = jnp.logical_and(lane >= first, lane < first + count)
    projection = jnp.where(inside, products / all_panels, 0.0)
    square = jnp.sum(jnp.where(lane == first + count, products, 0.0), axis=1, keepdims=True)
    index = iota((LANES, total.shape[1]), 1)
    which = iota((LANES, total.shape[1]), 0) - first
    many = jnp.broadcast_to(projection, (8, LANES))
    outer = dot(many, ones_where(index % count == which, jnp.float32), precision=HIGHEST)
    shifted = (index + index // count) % count == which
    inner = dot(many, ones_where(shifted, jnp.float32), precision=HIGHEST)
    diagonal = iota(total.shape, 1) // count
    once = jnp.logical_or(diagonal == 0, diagonal == count // 2)
    gram = jnp.where(diagonal <= count // 2, total * jnp.where(once, 1.0, 2.0), 0.0)
    squares = (
        square
        - 2.0 * jnp.sum(projection * products, axis=1, keepdims=True)
        + jnp.sum(gram * outer[:1] * inner[:1], axis=1, keepdims=True)
    )
    new_norm = jnp.sqrt(squares / all_panels + 1e-06)
    remainder = image_ref[...]
    for k in range(count):
        remainder = remainder - projection[:, first + k : first + k + 1] * basis_ref[k, 0]
    next_ref[0] = remainder / new_norm
    column = jnp.where(lane == first + count, new_norm, projection)
    hessenberg_ref[...] = column[:, first : first + count + 1]


def exchange(rows, axes):
    return lax.all_to_all(rows, axes, 0, 0)


def swapped(value, first):
    count = lax.axis_size(CL)
    route = []
    for i in range(first, count - 1, 2):
        route += [(i, i + 1), (i + 1, i)]
    return lax.ppermute(value, CL, route)


def f32(*shape):
    return jax.ShapeDtypeStruct(shape, jnp.float32)


def bf16(*shape):
    return jax.ShapeDtypeStruct(shape, jnp.bfloat16)


def on_device(
    basis,
    near_blocks,
    near_list,
    source_basis,
    target_basis,
    coupling,
    far_target,
    far_source,
    far_count,
):
    count, _, clusters, panels = basis.shape
    ranks = source_basis.shape[2]
    slots = coupling.shape[1]
    owners = lax.axis_size(CL)
    width = clusters * ranks
    packed = 2 * LANES

    sent, current, targets = pl.pallas_call(
        expand_kernel,
        in_specs=[HBM, HBM, HBM],
        out_specs=[VMEM, VMEM, SMEM],
        out_shape=[
            bf16(owners, width // LANES, LANES),
            bf16(clusters, panels),
            jax.ShapeDtypeStruct((1, LANES), jnp.int32),
        ],
        scratch_shapes=[
            pltpu.VMEM((clusters, panels), jnp.float32),
            pltpu.VMEM((clusters, ranks, panels), jnp.bfloat16),
            pltpu.SemaphoreType.DMA((3,)),
        ],
        name="expand",
    )(basis, source_basis, far_target)
    expansions = exchange(sent, CL)
    current, targets, sources = pl.pallas_call(
        relay_kernel,
        in_specs=[VMEM, VMEM, VMEM, ANY],
        out_specs=[VMEM] * 3,
        out_shape=[
            bf16(clusters, panels),
            jax.ShapeDtypeStruct(targets.shape, jnp.int32),
            jax.ShapeDtypeStruct(far_source.shape, jnp.int32),
        ],
        compiler_params=SMALL,
        cost_estimate=pl.CostEstimate(flops=0, bytes_accessed=1 << 26, transcendentals=0),
        name="relay",
    )(current, targets, far_source, sent)
    other = swapped(current, 1)
    pair = swapped(current, 0)
    even = lax.axis_index("core") == 0
    near_ids = near_list[0]
    mirrored = (2 - near_ids // clusters) * clusters + near_ids % clusters
    near_ids = jnp.where(even, mirrored, near_ids)

    sent, held = pl.pallas_call(
        lambda *refs: far_kernel(clusters, owners, *refs),
        in_specs=[SMEM, SMEM, SMEM, VMEM, VMEM, VMEM],
        out_specs=[VMEM, VMEM],
        out_shape=[bf16(owners, width // LANES, LANES), bf16(clusters, panels)],
        compiler_params=SMALL,
        name="far",
    )(sources, targets, far_count, expansions, coupling, current)
    arrived = exchange(sent, CL)

    window = jnp.concatenate([pair, held, other], axis=0)
    near = jnp.einsum(
        "tkij,tkj->ti", near_blocks[0], window[near_ids], preferred_element_type=jnp.float32
    )
    gram = pl.pallas_call(
        gram_kernel,
        in_specs=[VMEM, ANY],
        out_specs=VMEM,
        out_shape=f32(1, packed),
        compiler_params=SMALL,
        name="gram",
    )(basis, held)
    image, sent = pl.pallas_call(
        lambda *refs: image_kernel(owners, *refs),
        in_specs=[VMEM] * 5,
        out_specs=[VMEM] * 2,
        out_shape=[f32(clusters, panels), f32(lax.axis_size(ROW), 1, packed)],
        compiler_params=SMALL,
        name="image",
    )(basis, target_basis, arrived, near, gram)
    sent = pl.pallas_call(
        total_kernel,
        in_specs=[VMEM],
        out_specs=VMEM,
        out_shape=f32(lax.axis_size(COLUMN), 1, packed),
        compiler_params=SMALL,
        name="total",
    )(exchange(sent, ROW))
    all_panels = float(owners * lax.axis_size("grp") * clusters * panels)
    next_vector, hessenberg = pl.pallas_call(
        lambda *refs: final_kernel(all_panels, *refs),
        in_specs=[VMEM] * 3,
        out_specs=[VMEM] * 2,
        out_shape=[f32(1, clusters, panels), f32(1, count + 1)],
        compiler_params=SMALL,
        name="final",
    )(basis, image, exchange(sent, COLUMN))
    return (next_vector, hessenberg.reshape(count + 1))


def solution(mesh):
    torus = Mesh(mesh.devices.reshape(8, 8, 2, mesh.shape["grp"]), (*CL, "grp"))
    in_specs = (
        P(None, "grp", CL, None),
        P("grp", CL, None, None, None),
        P("grp", CL, None),
        P("grp", CL, None, None),
        P("grp", CL, None, None),
        P("grp", CL, None),
        P("grp", None),
        P("grp", CL),
        P("grp", CL),
    )
    return jax.shard_map(
        on_device,
        mesh=torus,
        in_specs=in_specs,
        out_specs=(P("grp", CL, None), P()),
        check_vma=False,
    )
```

```python
import jax
import jax.numpy as jnp
from jax import lax
from jax.experimental import pallas as pl
from jax.experimental.pallas import tpu as pltpu
from jax.sharding import Mesh
from jax.sharding import PartitionSpec as P

CL = ("z", "x", "core")
ROW = ("x", "core")
COLUMN = ("z", "grp")
HIGHEST = lax.Precision.HIGHEST
LANES = 128
SHARERS = 8
FIRST, LAST = -2, 3

SMALL = pltpu.CompilerParams(vmem_limit_bytes=4 * 1024 * 1024)
VMEM = pl.BlockSpec(memory_space=pltpu.VMEM)
ANY = pl.BlockSpec(memory_space=pl.ANY)
HBM = pl.BlockSpec(memory_space=pltpu.HBM)
SMEM = pl.BlockSpec(memory_space=pltpu.SMEM)


def iota(shape, dim):
    return lax.broadcasted_iota(jnp.int32, shape, dim)


def dot(a, b, contract=((1,), (0,)), precision=None):
    return lax.dot_general(
        a, b, (contract, ((), ())), precision=precision, preferred_element_type=jnp.float32
    )


def ones_where(mask, dtype):
    return jnp.where(mask, 1.0, 0.0).astype(dtype)


def position():
    return lax.axis_index("z") * 16 + lax.axis_index("x") * 2 + lax.axis_index("core")


def relay_kernel(tile_ref, after_ref, relayed_ref):
    relayed_ref[...] = tile_ref[...]


def expand_kernel(
    basis_ref,
    source_ref,
    target_ref,
    slot_ref,
    sent_ref,
    current_ref,
    window_ref,
    sources_ref,
    tile_ref,
    matrix_ref,
    semaphores,
):
    count, _, clusters, panels = basis_ref.shape
    ranks = source_ref.shape[2]
    width = clusters * ranks
    first = pl.multiple_of(position() // SHARERS * LANES, LANES)
    copies = [
        pltpu.make_async_copy(basis_ref.at[count - 1, 0], tile_ref, semaphores.at[0]),
        pltpu.make_async_copy(source_ref.at[0], matrix_ref, semaphores.at[1]),
        pltpu.make_async_copy(target_ref.at[:, pl.ds(first, LANES)], window_ref, semaphores.at[2]),
        pltpu.make_async_copy(slot_ref, sources_ref, semaphores.at[3]),
    ]
    for copy in copies:
        copy.start()
    copies[0].wait()
    current = tile_ref[...].astype(jnp.bfloat16)
    current_ref[...] = current
    copies[1].wait()
    every = dot(current, matrix_ref[...].reshape(width, panels), ((1,), (1,)))
    own = iota((clusters, width), 1) // ranks == iota((clusters, width), 0)
    row = jnp.sum(jnp.where(own, every, 0.0), axis=0, keepdims=True)
    pieces = [row[:, i : i + LANES] for i in range(0, width, LANES)]
    tile = jnp.concatenate(pieces, axis=0).astype(jnp.bfloat16)
    sent_ref[...] = jnp.broadcast_to(tile[None], sent_ref.shape)
    copies[2].wait()
    copies[3].wait()


def far_kernel(
    clusters,
    owners,
    source_ref,
    target_ref,
    count_ref,
    expansion_ref,
    coupling_ref,
    current_ref,
    sent_ref,
    held_ref,
):
    held_ref[...] = current_ref[...]
    slots = coupling_ref.shape[1]
    width = expansion_ref.shape[1] * LANES
    ranks = width // clusters
    groups = LANES // ranks
    parts = ranks // groups
    me = position()
    lane_cluster = iota((1, width), 1) // ranks
    tile = expansion_ref.shape[1:]
    place = iota(tile, 0) * groups + iota(tile, 1) // ranks
    picked, targets = [], []
    for b in range(slots):
        source = source_ref[0, b]
        rows = expansion_ref[source // clusters].astype(jnp.float32)
        rows = jnp.where(place == source % clusters, rows, 0.0)
        picked.append(jnp.sum(rows, axis=0, keepdims=True))
        target = jnp.where(b < count_ref[0, 0], target_ref[0, lax.rem(me, SHARERS) * slots + b], -1)
        targets.append(jnp.full((1, width), target, jnp.int32))
    picked = jnp.concatenate(picked, axis=0).astype(jnp.bfloat16)
    targets = jnp.concatenate(targets, axis=0)
    spread = iota((LANES, LANES), 0) % ranks == iota((LANES, LANES), 1) % ranks
    vector = dot(picked, ones_where(spread, jnp.bfloat16))
    coupling = coupling_ref[0].astype(jnp.float32)
    high, low = [], []
    for q in range(parts):
        product = coupling[:, q * LANES : (q + 1) * LANES] * vector
        top = product.astype(jnp.bfloat16)
        high.append(top)
        low.append((product - top.astype(jnp.float32)).astype(jnp.bfloat16))
    gather = iota((LANES, width), 0) // ranks == iota((LANES, width), 1) % groups
    sums = dot(jnp.concatenate(high + low, axis=0), ones_where(gather, jnp.bfloat16))
    part = (iota((slots, width), 1) % ranks) // groups
    term = jnp.zeros((slots, width), jnp.float32)
    for q in range(parts):
        value = sums[q * slots : (q + 1) * slots] + sums[(parts + q) * slots : (parts + q + 1) * slots]
        term = jnp.where(part == q, value, term)
    sent_ref[...] = jnp.zeros_like(sent_ref)

    def send(owner):
        mine = targets == owner * clusters + lane_cluster
        row = jnp.sum(jnp.where(mine, term, 0.0), axis=0, keepdims=True)
        pieces = [row[:, i : i + LANES] for i in range(0, width, LANES)]
        sent_ref[owner] = jnp.concatenate(pieces, axis=0).astype(jnp.bfloat16)

    for step in range(FIRST, LAST + 1):
        owner = me + step

        @pl.when(jnp.logical_and(owner >= 0, owner < owners))
        def _():
            send(owner)

    send(lax.rem(me + owners // 2, owners))


def kept(count):
    return count * (count // 2 + 1)


def gram_kernel(basis_ref, after_ref, gram_ref):
    count, _, clusters, _ = basis_ref.shape
    gram = jnp.zeros((count, count), jnp.float32)
    for c in range(clusters):
        rows = basis_ref[:, 0, c, :]
        gram = gram + dot(rows, rows, ((1,), (1,)), HIGHEST)
    lane = iota((count, gram_ref.shape[1]), 1)
    row = iota((count, gram_ref.shape[1]), 0)
    pick = jnp.logical_and((lane + lane // count) % count == row, lane < kept(count))
    rows = dot(gram, ones_where(pick, jnp.float32), precision=HIGHEST)
    gram_ref[...] = jnp.sum(jnp.where(lane % count == row, rows, 0.0), axis=0, keepdims=True)


def image_kernel(owners, basis_ref, target_ref, arrived_ref, near_ref, gram_ref, image_ref, sent_ref):
    count = basis_ref.shape[0]
    clusters, panels = near_ref.shape
    ranks = target_ref.shape[2]
    width = clusters * ranks
    me = position()
    coupled = arrived_ref[lax.rem(me + owners // 2, owners)].astype(jnp.float32)
    for step in range(-LAST, -FIRST + 1):
        owner = me + step
        inside = jnp.logical_and(owner >= 0, owner < owners)
        value = arrived_ref[jnp.clip(owner, 0, owners - 1)].astype(jnp.float32)
        coupled = coupled + jnp.where(inside, value, 0.0)
    coupled = jnp.concatenate([coupled[i : i + 1] for i in range(coupled.shape[0])], axis=1)
    own = iota((clusters, width), 1) // ranks == iota((clusters, width), 0)
    spread = jnp.where(own, coupled, 0.0).astype(jnp.bfloat16)
    far = dot(spread, target_ref[0].reshape(width, panels))
    image = 0.5 * basis_ref[count - 1, 0] + near_ref[...] + far
    image_ref[...] = image
    first = kept(count) % LANES
    rows = [jnp.zeros((first, panels), jnp.float32)]
    rows += [jnp.sum(basis_ref[k, 0] * image, axis=0, keepdims=True) for k in range(count)]
    rows.append(jnp.sum(image * image, axis=0, keepdims=True))
    rows.append(jnp.zeros((LANES - first - count - 1, panels), jnp.float32))
    products = dot(
        jnp.ones((8, panels), jnp.float32), jnp.concatenate(rows, axis=0), ((1,), (1,)), HIGHEST
    )
    gram = gram_ref[...]
    row = jnp.concatenate([gram[:, :LANES], gram[:, LANES:] + products[:1]], axis=1)
    sent_ref[...] = jnp.broadcast_to(row[None], sent_ref.shape)


def total_kernel(arrived_ref, sent_ref):
    sent_ref[...] = jnp.broadcast_to(
        jnp.sum(arrived_ref[...], axis=0, keepdims=True), sent_ref.shape
    )


def final_kernel(all_panels, basis_ref, image_ref, arrived_ref, next_ref, hessenberg_ref):
    count = basis_ref.shape[0]
    first = kept(count) % LANES
    total = jnp.sum(arrived_ref[...], axis=0)
    products = total[:, LANES:]
    lane = iota((1, LANES), 1)
    inside = jnp.logical_and(lane >= first, lane < first + count)
    projection = jnp.where(inside, products / all_panels, 0.0)
    square = jnp.sum(jnp.where(lane == first + count, products, 0.0), axis=1, keepdims=True)
    index = iota((LANES, total.shape[1]), 1)
    which = iota((LANES, total.shape[1]), 0) - first
    many = jnp.broadcast_to(projection, (8, LANES))
    outer = dot(many, ones_where(index % count == which, jnp.float32), precision=HIGHEST)
    shifted = (index + index // count) % count == which
    inner = dot(many, ones_where(shifted, jnp.float32), precision=HIGHEST)
    diagonal = iota(total.shape, 1) // count
    once = jnp.logical_or(diagonal == 0, diagonal == count // 2)
    gram = jnp.where(diagonal <= count // 2, total * jnp.where(once, 1.0, 2.0), 0.0)
    squares = (
        square
        - 2.0 * jnp.sum(projection * products, axis=1, keepdims=True)
        + jnp.sum(gram * outer[:1] * inner[:1], axis=1, keepdims=True)
    )
    new_norm = jnp.sqrt(squares / all_panels + 1e-06)
    remainder = image_ref[...]
    for k in range(count):
        remainder = remainder - projection[:, first + k : first + k + 1] * basis_ref[k, 0]
    next_ref[0] = remainder / new_norm
    column = jnp.where(lane == first + count, new_norm, projection)
    hessenberg_ref[...] = column[:, first : first + count + 1]


def exchange(rows, axes):
    return lax.all_to_all(rows, axes, 0, 0)


def swapped(value, first):
    count = lax.axis_size(CL)
    route = []
    for i in range(first, count - 1, 2):
        route += [(i, i + 1), (i + 1, i)]
    return lax.ppermute(value, CL, route)


def f32(*shape):
    return jax.ShapeDtypeStruct(shape, jnp.float32)


def bf16(*shape):
    return jax.ShapeDtypeStruct(shape, jnp.bfloat16)


def on_device(
    basis,
    near_blocks,
    near_list,
    source_basis,
    target_basis,
    coupling,
    far_target,
    far_source,
    far_count,
):
    count, _, clusters, panels = basis.shape
    ranks = source_basis.shape[2]
    slots = coupling.shape[1]
    owners = lax.axis_size(CL)
    width = clusters * ranks
    packed = 2 * LANES

    sent, current, targets, sources = pl.pallas_call(
        expand_kernel,
        in_specs=[HBM] * 4,
        out_specs=[VMEM] * 4,
        out_shape=[
            bf16(owners, width // LANES, LANES),
            pltpu.VMEM((clusters, panels), jnp.bfloat16),
            pltpu.VMEM((1, LANES), jnp.int32),
            pltpu.VMEM(far_source.shape, jnp.int32),
        ],
        scratch_shapes=[
            pltpu.VMEM((clusters, panels), jnp.float32),
            pltpu.VMEM((clusters, ranks, panels), jnp.bfloat16),
            pltpu.SemaphoreType.DMA((4,)),
        ],
        name="expand",
    )(basis, source_basis, far_target, far_source)
    expansions = exchange(sent, CL)
    current = pl.pallas_call(
        relay_kernel,
        in_specs=[VMEM, ANY],
        out_specs=VMEM,
        out_shape=bf16(clusters, panels),
        compiler_params=SMALL,
        cost_estimate=pl.CostEstimate(flops=0, bytes_accessed=1 << 26, transcendentals=0),
        name="relay",
    )(current, sent)
    other = swapped(current, 1)
    pair = swapped(current, 0)
    even = lax.axis_index("core") == 0
    near_ids = near_list[0]
    mirrored = (2 - near_ids // clusters) * clusters + near_ids % clusters
    near_ids = jnp.where(even, mirrored, near_ids)

    sent, held = pl.pallas_call(
        lambda *refs: far_kernel(clusters, owners, *refs),
        in_specs=[SMEM, SMEM, SMEM, VMEM, VMEM, VMEM],
        out_specs=[VMEM, VMEM],
        out_shape=[bf16(owners, width // LANES, LANES), bf16(clusters, panels)],
        compiler_params=SMALL,
        name="far",
    )(sources, targets, far_count, expansions, coupling, current)
    arrived = exchange(sent, CL)

    window = jnp.concatenate([pair, held, other], axis=0)
    near = jnp.einsum(
        "tkij,tkj->ti", near_blocks[0], window[near_ids], preferred_element_type=jnp.float32
    )
    gram = pl.pallas_call(
        gram_kernel,
        in_specs=[VMEM, ANY],
        out_specs=VMEM,
        out_shape=f32(1, packed),
        compiler_params=SMALL,
        name="gram",
    )(basis, held)
    image, sent = pl.pallas_call(
        lambda *refs: image_kernel(owners, *refs),
        in_specs=[VMEM] * 5,
        out_specs=[VMEM] * 2,
        out_shape=[f32(clusters, panels), f32(lax.axis_size(ROW), 1, packed)],
        compiler_params=SMALL,
        name="image",
    )(basis, target_basis, arrived, near, gram)
    sent = pl.pallas_call(
        total_kernel,
        in_specs=[VMEM],
        out_specs=VMEM,
        out_shape=f32(lax.axis_size(COLUMN), 1, packed),
        compiler_params=SMALL,
        name="total",
    )(exchange(sent, ROW))
    all_panels = float(owners * lax.axis_size("grp") * clusters * panels)
    next_vector, hessenberg = pl.pallas_call(
        lambda *refs: final_kernel(all_panels, *refs),
        in_specs=[VMEM] * 3,
        out_specs=[VMEM] * 2,
        out_shape=[f32(1, clusters, panels), f32(1, count + 1)],
        compiler_params=SMALL,
        name="final",
    )(basis, image, exchange(sent, COLUMN))
    return (next_vector, hessenberg.reshape(count + 1))


def solution(mesh):
    torus = Mesh(mesh.devices.reshape(8, 8, 2, mesh.shape["grp"]), (*CL, "grp"))
    in_specs = (
        P(None, "grp", CL, None),
        P("grp", CL, None, None, None),
        P("grp", CL, None),
        P("grp", CL, None, None),
        P("grp", CL, None, None),
        P("grp", CL, None),
        P("grp", None),
        P("grp", CL),
        P("grp", CL),
    )
    return jax.shard_map(
        on_device,
        mesh=torus,
        in_specs=in_specs,
        out_specs=(P("grp", CL, None), P()),
        check_vma=False,
    )
```

```python
import jax
import jax.numpy as jnp
from jax import lax
from jax.experimental import pallas as pl
from jax.experimental.pallas import tpu as pltpu
from jax.sharding import Mesh
from jax.sharding import PartitionSpec as P

CL = ("z", "x", "core")
ROW = ("x", "core")
COLUMN = ("z", "grp")
HIGHEST = lax.Precision.HIGHEST
LANES = 128
SHARERS = 8
FIRST, LAST = -2, 3

SMALL = pltpu.CompilerParams(vmem_limit_bytes=4 * 1024 * 1024)
VMEM = pl.BlockSpec(memory_space=pltpu.VMEM)
ANY = pl.BlockSpec(memory_space=pl.ANY)
HBM = pl.BlockSpec(memory_space=pltpu.HBM)
SMEM = pl.BlockSpec(memory_space=pltpu.SMEM)


def iota(shape, dim):
    return lax.broadcasted_iota(jnp.int32, shape, dim)


def dot(a, b, contract=((1,), (0,)), precision=None):
    return lax.dot_general(
        a, b, (contract, ((), ())), precision=precision, preferred_element_type=jnp.float32
    )


def ones_where(mask, dtype):
    return jnp.where(mask, 1.0, 0.0).astype(dtype)


def position():
    return lax.axis_index("z") * 16 + lax.axis_index("x") * 2 + lax.axis_index("core")


def relay_kernel(tile_ref, after_ref, relayed_ref):
    relayed_ref[...] = tile_ref[...]


def expand_kernel(
    basis_ref,
    source_ref,
    target_ref,
    slot_ref,
    sent_ref,
    current_ref,
    window_ref,
    sources_ref,
    tile_ref,
    matrix_ref,
    semaphores,
):
    count, _, clusters, panels = basis_ref.shape
    ranks = source_ref.shape[2]
    width = clusters * ranks
    first = pl.multiple_of(position() // SHARERS * LANES, LANES)
    copies = [
        pltpu.make_async_copy(basis_ref.at[count - 1, 0], tile_ref, semaphores.at[0]),
        pltpu.make_async_copy(source_ref.at[0], matrix_ref, semaphores.at[1]),
        pltpu.make_async_copy(target_ref.at[:, pl.ds(first, LANES)], window_ref, semaphores.at[2]),
        pltpu.make_async_copy(slot_ref, sources_ref, semaphores.at[3]),
    ]
    for copy in copies:
        copy.start()
    copies[0].wait()
    current = tile_ref[...].astype(jnp.bfloat16)
    current_ref[...] = current
    copies[1].wait()
    every = dot(current, matrix_ref[...].reshape(width, panels), ((1,), (1,)))
    own = iota((clusters, width), 1) // ranks == iota((clusters, width), 0)
    row = jnp.sum(jnp.where(own, every, 0.0), axis=0, keepdims=True)
    pieces = [row[:, i : i + LANES] for i in range(0, width, LANES)]
    tile = jnp.concatenate(pieces, axis=0).astype(jnp.bfloat16)
    sent_ref[...] = jnp.broadcast_to(tile[None], sent_ref.shape)
    copies[2].wait()
    copies[3].wait()


def far_kernel(
    clusters,
    owners,
    source_ref,
    target_ref,
    count_ref,
    expansion_ref,
    coupling_ref,
    current_ref,
    sent_ref,
    held_ref,
):
    held_ref[...] = current_ref[...]
    slots = coupling_ref.shape[1]
    width = expansion_ref.shape[1] * LANES
    ranks = width // clusters
    groups = LANES // ranks
    parts = ranks // groups
    me = position()
    lane_cluster = iota((1, width), 1) // ranks
    tile = expansion_ref.shape[1:]
    place = iota(tile, 0) * groups + iota(tile, 1) // ranks
    picked, targets = [], []
    for b in range(slots):
        source = source_ref[0, b]
        rows = expansion_ref[source // clusters].astype(jnp.float32)
        rows = jnp.where(place == source % clusters, rows, 0.0)
        picked.append(jnp.sum(rows, axis=0, keepdims=True))
        target = jnp.where(b < count_ref[0, 0], target_ref[0, lax.rem(me, SHARERS) * slots + b], -1)
        targets.append(jnp.full((1, width), target, jnp.int32))
    picked = jnp.concatenate(picked, axis=0).astype(jnp.bfloat16)
    targets = jnp.concatenate(targets, axis=0)
    spread = iota((LANES, LANES), 0) % ranks == iota((LANES, LANES), 1) % ranks
    vector = dot(picked, ones_where(spread, jnp.bfloat16))
    coupling = coupling_ref[0].astype(jnp.float32)
    high, low = [], []
    for q in range(parts):
        product = coupling[:, q * LANES : (q + 1) * LANES] * vector
        top = product.astype(jnp.bfloat16)
        high.append(top)
        low.append((product - top.astype(jnp.float32)).astype(jnp.bfloat16))
    gather = iota((LANES, width), 0) // ranks == iota((LANES, width), 1) % groups
    sums = dot(jnp.concatenate(high + low, axis=0), ones_where(gather, jnp.bfloat16))
    part = (iota((slots, width), 1) % ranks) // groups
    term = jnp.zeros((slots, width), jnp.float32)
    for q in range(parts):
        value = sums[q * slots : (q + 1) * slots] + sums[(parts + q) * slots : (parts + q + 1) * slots]
        term = jnp.where(part == q, value, term)
    sent_ref[...] = jnp.zeros_like(sent_ref)

    def send(owner):
        mine = targets == owner * clusters + lane_cluster
        row = jnp.sum(jnp.where(mine, term, 0.0), axis=0, keepdims=True)
        pieces = [row[:, i : i + LANES] for i in range(0, width, LANES)]
        sent_ref[owner] = jnp.concatenate(pieces, axis=0).astype(jnp.bfloat16)

    for step in range(FIRST, LAST + 1):
        owner = me + step

        @pl.when(jnp.logical_and(owner >= 0, owner < owners))
        def _():
            send(owner)

    send(lax.rem(me + owners // 2, owners))


def kept(count):
    return count * (count // 2 + 1)


def gram_kernel(basis_ref, after_ref, gram_ref):
    count, _, clusters, _ = basis_ref.shape
    gram = jnp.zeros((count, count), jnp.float32)
    for c in range(clusters):
        rows = basis_ref[:, 0, c, :]
        gram = gram + dot(rows, rows, ((1,), (1,)), HIGHEST)
    lane = iota((count, gram_ref.shape[1]), 1)
    row = iota((count, gram_ref.shape[1]), 0)
    pick = jnp.logical_and((lane + lane // count) % count == row, lane < kept(count))
    rows = dot(gram, ones_where(pick, jnp.float32), precision=HIGHEST)
    gram_ref[...] = jnp.sum(jnp.where(lane % count == row, rows, 0.0), axis=0, keepdims=True)


def image_kernel(owners, basis_ref, target_ref, arrived_ref, near_ref, gram_ref, image_ref, sent_ref):
    count = basis_ref.shape[0]
    clusters, panels = near_ref.shape
    ranks = target_ref.shape[2]
    width = clusters * ranks
    me = position()
    coupled = arrived_ref[lax.rem(me + owners // 2, owners)].astype(jnp.float32)
    for step in range(-LAST, -FIRST + 1):
        owner = me + step
        inside = jnp.logical_and(owner >= 0, owner < owners)
        value = arrived_ref[jnp.clip(owner, 0, owners - 1)].astype(jnp.float32)
        coupled = coupled + jnp.where(inside, value, 0.0)
    coupled = jnp.concatenate([coupled[i : i + 1] for i in range(coupled.shape[0])], axis=1)
    own = iota((clusters, width), 1) // ranks == iota((clusters, width), 0)
    spread = jnp.where(own, coupled, 0.0).astype(jnp.bfloat16)
    far = dot(spread, target_ref[0].reshape(width, panels))
    image = 0.5 * basis_ref[count - 1, 0] + near_ref[...] + far
    image_ref[...] = image
    first = kept(count) % LANES
    rows = [jnp.zeros((first, panels), jnp.float32)]
    rows += [jnp.sum(basis_ref[k, 0] * image, axis=0, keepdims=True) for k in range(count)]
    rows.append(jnp.sum(image * image, axis=0, keepdims=True))
    rows.append(jnp.zeros((LANES - first - count - 1, panels), jnp.float32))
    products = dot(
        jnp.ones((8, panels), jnp.float32), jnp.concatenate(rows, axis=0), ((1,), (1,)), HIGHEST
    )
    gram = gram_ref[...]
    row = jnp.concatenate([gram[:, :LANES], gram[:, LANES:] + products[:1]], axis=1)
    sent_ref[...] = jnp.broadcast_to(row[None], sent_ref.shape)


def total_kernel(arrived_ref, sent_ref):
    sent_ref[...] = jnp.broadcast_to(
        jnp.sum(arrived_ref[...], axis=0, keepdims=True), sent_ref.shape
    )


def final_kernel(all_panels, basis_ref, image_ref, arrived_ref, next_ref, hessenberg_ref):
    count = basis_ref.shape[0]
    first = kept(count) % LANES
    total = jnp.sum(arrived_ref[...], axis=0)
    products = total[:, LANES:]
    lane = iota((1, LANES), 1)
    inside = jnp.logical_and(lane >= first, lane < first + count)
    projection = jnp.where(inside, products / all_panels, 0.0)
    square = jnp.sum(jnp.where(lane == first + count, products, 0.0), axis=1, keepdims=True)
    index = iota((LANES, total.shape[1]), 1)
    which = iota((LANES, total.shape[1]), 0) - first
    many = jnp.broadcast_to(projection, (8, LANES))
    outer = dot(many, ones_where(index % count == which, jnp.float32), precision=HIGHEST)
    shifted = (index + index // count) % count == which
    inner = dot(many, ones_where(shifted, jnp.float32), precision=HIGHEST)
    diagonal = iota(total.shape, 1) // count
    once = jnp.logical_or(diagonal == 0, diagonal == count // 2)
    gram = jnp.where(diagonal <= count // 2, total * jnp.where(once, 1.0, 2.0), 0.0)
    squares = (
        square
        - 2.0 * jnp.sum(projection * products, axis=1, keepdims=True)
        + jnp.sum(gram * outer[:1] * inner[:1], axis=1, keepdims=True)
    )
    new_norm = jnp.sqrt(squares / all_panels + 1e-06)
    remainder = image_ref[...]
    for k in range(count):
        remainder = remainder - projection[:, first + k : first + k + 1] * basis_ref[k, 0]
    next_ref[0] = remainder / new_norm
    column = jnp.where(lane == first + count, new_norm, projection)
    hessenberg_ref[...] = column[:, first : first + count + 1]


def exchange(rows, axes):
    return lax.all_to_all(rows, axes, 0, 0)


def swapped(value, first):
    count = lax.axis_size(CL)
    route = []
    for i in range(first, count - 1, 2):
        route += [(i, i + 1), (i + 1, i)]
    return lax.ppermute(value, CL, route)


def f32(*shape):
    return jax.ShapeDtypeStruct(shape, jnp.float32)


def bf16(*shape):
    return jax.ShapeDtypeStruct(shape, jnp.bfloat16)


def on_device(
    basis,
    near_blocks,
    near_list,
    source_basis,
    target_basis,
    coupling,
    far_target,
    far_source,
    far_count,
):
    count, _, clusters, panels = basis.shape
    ranks = source_basis.shape[2]
    slots = coupling.shape[1]
    owners = lax.axis_size(CL)
    width = clusters * ranks
    packed = 2 * LANES

    sent, current, targets, sources = pl.pallas_call(
        expand_kernel,
        in_specs=[HBM] * 4,
        out_specs=[VMEM] * 4,
        out_shape=[
            bf16(owners, width // LANES, LANES),
            pltpu.VMEM((clusters, panels), jnp.bfloat16),
            pltpu.VMEM((1, LANES), jnp.int32),
            pltpu.VMEM(far_source.shape, jnp.int32),
        ],
        scratch_shapes=[
            pltpu.VMEM((clusters, panels), jnp.float32),
            pltpu.VMEM((clusters, ranks, panels), jnp.bfloat16),
            pltpu.SemaphoreType.DMA((4,)),
        ],
        name="expand",
    )(basis, source_basis, far_target, far_source)
    expansions = exchange(sent, CL)
    relay = pl.pallas_call(
        relay_kernel,
        in_specs=[VMEM, ANY],
        out_specs=VMEM,
        out_shape=bf16(clusters, panels),
        compiler_params=SMALL,
        cost_estimate=pl.CostEstimate(flops=0, bytes_accessed=1 << 26, transcendentals=0),
        name="relay",
    )
    current = relay(current, sent)
    pair = swapped(current, 0)
    other = swapped(relay(current, sent), 1)
    even = lax.axis_index("core") == 0
    near_ids = near_list[0]
    mirrored = (2 - near_ids // clusters) * clusters + near_ids % clusters
    near_ids = jnp.where(even, mirrored, near_ids)

    sent, held = pl.pallas_call(
        lambda *refs: far_kernel(clusters, owners, *refs),
        in_specs=[SMEM, SMEM, SMEM, VMEM, VMEM, VMEM],
        out_specs=[VMEM, VMEM],
        out_shape=[bf16(owners, width // LANES, LANES), bf16(clusters, panels)],
        compiler_params=SMALL,
        name="far",
    )(sources, targets, far_count, expansions, coupling, current)
    arrived = exchange(sent, CL)

    window = jnp.concatenate([pair, held, other], axis=0)
    near = jnp.einsum(
        "tkij,tkj->ti", near_blocks[0], window[near_ids], preferred_element_type=jnp.float32
    )
    gram = pl.pallas_call(
        gram_kernel,
        in_specs=[VMEM, ANY],
        out_specs=VMEM,
        out_shape=f32(1, packed),
        compiler_params=SMALL,
        name="gram",
    )(basis, near)
    image, sent = pl.pallas_call(
        lambda *refs: image_kernel(owners, *refs),
        in_specs=[VMEM] * 5,
        out_specs=[VMEM] * 2,
        out_shape=[f32(clusters, panels), f32(lax.axis_size(ROW), 1, packed)],
        compiler_params=SMALL,
        name="image",
    )(basis, target_basis, arrived, near, gram)
    sent = pl.pallas_call(
        total_kernel,
        in_specs=[VMEM],
        out_specs=VMEM,
        out_shape=f32(lax.axis_size(COLUMN), 1, packed),
        compiler_params=SMALL,
        name="total",
    )(exchange(sent, ROW))
    all_panels = float(owners * lax.axis_size("grp") * clusters * panels)
    next_vector, hessenberg = pl.pallas_call(
        lambda *refs: final_kernel(all_panels, *refs),
        in_specs=[VMEM] * 3,
        out_specs=[VMEM] * 2,
        out_shape=[f32(1, clusters, panels), f32(1, count + 1)],
        compiler_params=SMALL,
        name="final",
    )(basis, image, exchange(sent, COLUMN))
    return (next_vector, hessenberg.reshape(count + 1))


def solution(mesh):
    torus = Mesh(mesh.devices.reshape(8, 8, 2, mesh.shape["grp"]), (*CL, "grp"))
    in_specs = (
        P(None, "grp", CL, None),
        P("grp", CL, None, None, None),
        P("grp", CL, None),
        P("grp", CL, None, None),
        P("grp", CL, None, None),
        P("grp", CL, None),
        P("grp", None),
        P("grp", CL),
        P("grp", CL),
    )
    return jax.shard_map(
        on_device,
        mesh=torus,
        in_specs=in_specs,
        out_specs=(P("grp", CL, None), P()),
        check_vma=False,
    )
```

```python
import jax
import jax.numpy as jnp
from jax import lax
from jax.experimental import pallas as pl
from jax.experimental.pallas import tpu as pltpu
from jax.sharding import Mesh
from jax.sharding import PartitionSpec as P

CL = ("z", "x", "core")
ROW = ("x", "core")
COLUMN = ("z", "grp")
HIGHEST = lax.Precision.HIGHEST
LANES = 128
SHARERS = 8
FIRST, LAST = -2, 3

SMALL = pltpu.CompilerParams(vmem_limit_bytes=4 * 1024 * 1024)
VMEM = pl.BlockSpec(memory_space=pltpu.VMEM)
ANY = pl.BlockSpec(memory_space=pl.ANY)
HBM = pl.BlockSpec(memory_space=pltpu.HBM)
SMEM = pl.BlockSpec(memory_space=pltpu.SMEM)


def iota(shape, dim):
    return lax.broadcasted_iota(jnp.int32, shape, dim)


def dot(a, b, contract=((1,), (0,)), precision=None):
    return lax.dot_general(
        a, b, (contract, ((), ())), precision=precision, preferred_element_type=jnp.float32
    )


def ones_where(mask, dtype):
    return jnp.where(mask, 1.0, 0.0).astype(dtype)


def position():
    return lax.axis_index("z") * 16 + lax.axis_index("x") * 2 + lax.axis_index("core")


def relay_kernel(tile_ref, after_ref, relayed_ref):
    relayed_ref[...] = tile_ref[...]


def expand_kernel(
    basis_ref,
    source_ref,
    target_ref,
    slot_ref,
    sent_ref,
    current_ref,
    window_ref,
    sources_ref,
    tile_ref,
    matrix_ref,
    semaphores,
):
    count, _, clusters, panels = basis_ref.shape
    ranks = source_ref.shape[2]
    width = clusters * ranks
    first = pl.multiple_of(position() // SHARERS * LANES, LANES)
    copies = [
        pltpu.make_async_copy(basis_ref.at[count - 1, 0], tile_ref, semaphores.at[0]),
        pltpu.make_async_copy(source_ref.at[0], matrix_ref, semaphores.at[1]),
        pltpu.make_async_copy(target_ref.at[:, pl.ds(first, LANES)], window_ref, semaphores.at[2]),
        pltpu.make_async_copy(slot_ref, sources_ref, semaphores.at[3]),
    ]
    for copy in copies:
        copy.start()
    copies[0].wait()
    current = tile_ref[...].astype(jnp.bfloat16)
    current_ref[...] = current
    copies[1].wait()
    every = dot(current, matrix_ref[...].reshape(width, panels), ((1,), (1,)))
    own = iota((clusters, width), 1) // ranks == iota((clusters, width), 0)
    row = jnp.sum(jnp.where(own, every, 0.0), axis=0, keepdims=True)
    pieces = [row[:, i : i + LANES] for i in range(0, width, LANES)]
    tile = jnp.concatenate(pieces, axis=0).astype(jnp.bfloat16)
    sent_ref[...] = jnp.broadcast_to(tile[None], sent_ref.shape)
    copies[2].wait()
    copies[3].wait()


def far_kernel(
    clusters,
    owners,
    source_ref,
    target_ref,
    count_ref,
    expansion_ref,
    coupling_ref,
    current_ref,
    sent_ref,
    held_ref,
):
    held_ref[...] = current_ref[...]
    slots = coupling_ref.shape[1]
    width = expansion_ref.shape[1] * LANES
    ranks = width // clusters
    groups = LANES // ranks
    parts = ranks // groups
    me = position()
    lane_cluster = iota((1, width), 1) // ranks
    tile = expansion_ref.shape[1:]
    place = iota(tile, 0) * groups + iota(tile, 1) // ranks
    picked, targets = [], []
    for b in range(slots):
        source = source_ref[0, b]
        rows = expansion_ref[source // clusters].astype(jnp.float32)
        rows = jnp.where(place == source % clusters, rows, 0.0)
        picked.append(jnp.sum(rows, axis=0, keepdims=True))
        target = jnp.where(b < count_ref[0, 0], target_ref[0, lax.rem(me, SHARERS) * slots + b], -1)
        targets.append(jnp.full((1, width), target, jnp.int32))
    picked = jnp.concatenate(picked, axis=0).astype(jnp.bfloat16)
    targets = jnp.concatenate(targets, axis=0)
    spread = iota((LANES, LANES), 0) % ranks == iota((LANES, LANES), 1) % ranks
    vector = dot(picked, ones_where(spread, jnp.bfloat16))
    coupling = coupling_ref[0].astype(jnp.float32)
    high, low = [], []
    for q in range(parts):
        product = coupling[:, q * LANES : (q + 1) * LANES] * vector
        top = product.astype(jnp.bfloat16)
        high.append(top)
        low.append((product - top.astype(jnp.float32)).astype(jnp.bfloat16))
    gather = iota((LANES, width), 0) // ranks == iota((LANES, width), 1) % groups
    sums = dot(jnp.concatenate(high + low, axis=0), ones_where(gather, jnp.bfloat16))
    part = (iota((slots, width), 1) % ranks) // groups
    term = jnp.zeros((slots, width), jnp.float32)
    for q in range(parts):
        value = sums[q * slots : (q + 1) * slots] + sums[(parts + q) * slots : (parts + q + 1) * slots]
        term = jnp.where(part == q, value, term)
    sent_ref[...] = jnp.zeros_like(sent_ref)

    def send(owner):
        mine = targets == owner * clusters + lane_cluster
        row = jnp.sum(jnp.where(mine, term, 0.0), axis=0, keepdims=True)
        pieces = [row[:, i : i + LANES] for i in range(0, width, LANES)]
        sent_ref[owner] = jnp.concatenate(pieces, axis=0).astype(jnp.bfloat16)

    for step in range(FIRST, LAST + 1):
        owner = me + step

        @pl.when(jnp.logical_and(owner >= 0, owner < owners))
        def _():
            send(owner)

    send(lax.rem(me + owners // 2, owners))


def kept(count):
    return count * (count // 2 + 1)


def near_kernel(list_ref, pair_ref, held_ref, other_ref, blocks_ref, near_ref, window_ref):
    _, clusters, blocks, panels, _ = blocks_ref.shape
    for i, tile in enumerate((pair_ref, held_ref, other_ref)):
        window_ref[i * clusters : (i + 1) * clusters] = tile[...].astype(jnp.float32)
    even = lax.axis_index("core") == 0
    for t in range(clusters):
        rows = []
        for k in range(blocks):
            index = list_ref[k, t]
            mirrored = (2 - index // clusters) * clusters + index % clusters
            rows.append(window_ref[pl.ds(jnp.where(even, mirrored, index), 1), :])
        rows.append(jnp.zeros((8 - blocks, panels), jnp.float32))
        vectors = jnp.concatenate(rows, axis=0).astype(jnp.bfloat16)
        matrix = blocks_ref[0, t].reshape(blocks * panels, panels)
        every = dot(vectors, matrix, ((1,), (1,)))
        total = every[0:1, :panels]
        for k in range(1, blocks):
            total = total + every[k : k + 1, k * panels : (k + 1) * panels]
        near_ref[t : t + 1, :] = total


def gram_kernel(basis_ref, after_ref, gram_ref):
    count, _, clusters, _ = basis_ref.shape
    gram = jnp.zeros((count, count), jnp.float32)
    for c in range(clusters):
        rows = basis_ref[:, 0, c, :]
        gram = gram + dot(rows, rows, ((1,), (1,)), HIGHEST)
    lane = iota((count, gram_ref.shape[1]), 1)
    row = iota((count, gram_ref.shape[1]), 0)
    pick = jnp.logical_and((lane + lane // count) % count == row, lane < kept(count))
    rows = dot(gram, ones_where(pick, jnp.float32), precision=HIGHEST)
    gram_ref[...] = jnp.sum(jnp.where(lane % count == row, rows, 0.0), axis=0, keepdims=True)


def image_kernel(owners, basis_ref, target_ref, arrived_ref, near_ref, gram_ref, image_ref, sent_ref):
    count = basis_ref.shape[0]
    clusters, panels = near_ref.shape
    ranks = target_ref.shape[2]
    width = clusters * ranks
    me = position()
    coupled = arrived_ref[lax.rem(me + owners // 2, owners)].astype(jnp.float32)
    for step in range(-LAST, -FIRST + 1):
        owner = me + step
        inside = jnp.logical_and(owner >= 0, owner < owners)
        value = arrived_ref[jnp.clip(owner, 0, owners - 1)].astype(jnp.float32)
        coupled = coupled + jnp.where(inside, value, 0.0)
    coupled = jnp.concatenate([coupled[i : i + 1] for i in range(coupled.shape[0])], axis=1)
    own = iota((clusters, width), 1) // ranks == iota((clusters, width), 0)
    spread = jnp.where(own, coupled, 0.0).astype(jnp.bfloat16)
    far = dot(spread, target_ref[0].reshape(width, panels))
    image = 0.5 * basis_ref[count - 1, 0] + near_ref[...] + far
    image_ref[...] = image
    first = kept(count) % LANES
    rows = [jnp.zeros((first, panels), jnp.float32)]
    rows += [jnp.sum(basis_ref[k, 0] * image, axis=0, keepdims=True) for k in range(count)]
    rows.append(jnp.sum(image * image, axis=0, keepdims=True))
    rows.append(jnp.zeros((LANES - first - count - 1, panels), jnp.float32))
    products = dot(
        jnp.ones((8, panels), jnp.float32), jnp.concatenate(rows, axis=0), ((1,), (1,)), HIGHEST
    )
    gram = gram_ref[...]
    row = jnp.concatenate([gram[:, :LANES], gram[:, LANES:] + products[:1]], axis=1)
    sent_ref[...] = jnp.broadcast_to(row[None], sent_ref.shape)


def total_kernel(arrived_ref, sent_ref):
    sent_ref[...] = jnp.broadcast_to(
        jnp.sum(arrived_ref[...], axis=0, keepdims=True), sent_ref.shape
    )


def final_kernel(all_panels, basis_ref, image_ref, arrived_ref, next_ref, hessenberg_ref):
    count = basis_ref.shape[0]
    first = kept(count) % LANES
    total = jnp.sum(arrived_ref[...], axis=0)
    products = total[:, LANES:]
    lane = iota((1, LANES), 1)
    inside = jnp.logical_and(lane >= first, lane < first + count)
    projection = jnp.where(inside, products / all_panels, 0.0)
    square = jnp.sum(jnp.where(lane == first + count, products, 0.0), axis=1, keepdims=True)
    index = iota((LANES, total.shape[1]), 1)
    which = iota((LANES, total.shape[1]), 0) - first
    many = jnp.broadcast_to(projection, (8, LANES))
    outer = dot(many, ones_where(index % count == which, jnp.float32), precision=HIGHEST)
    shifted = (index + index // count) % count == which
    inner = dot(many, ones_where(shifted, jnp.float32), precision=HIGHEST)
    diagonal = iota(total.shape, 1) // count
    once = jnp.logical_or(diagonal == 0, diagonal == count // 2)
    gram = jnp.where(diagonal <= count // 2, total * jnp.where(once, 1.0, 2.0), 0.0)
    squares = (
        square
        - 2.0 * jnp.sum(projection * products, axis=1, keepdims=True)
        + jnp.sum(gram * outer[:1] * inner[:1], axis=1, keepdims=True)
    )
    new_norm = jnp.sqrt(squares / all_panels + 1e-06)
    remainder = image_ref[...]
    for k in range(count):
        remainder = remainder - projection[:, first + k : first + k + 1] * basis_ref[k, 0]
    next_ref[0] = remainder / new_norm
    column = jnp.where(lane == first + count, new_norm, projection)
    hessenberg_ref[...] = column[:, first : first + count + 1]


def exchange(rows, axes):
    return lax.all_to_all(rows, axes, 0, 0)


def swapped(value, first):
    count = lax.axis_size(CL)
    route = []
    for i in range(first, count - 1, 2):
        route += [(i, i + 1), (i + 1, i)]
    return lax.ppermute(value, CL, route)


def f32(*shape):
    return jax.ShapeDtypeStruct(shape, jnp.float32)


def bf16(*shape):
    return jax.ShapeDtypeStruct(shape, jnp.bfloat16)


def on_device(
    basis,
    near_blocks,
    near_list,
    source_basis,
    target_basis,
    coupling,
    far_target,
    far_source,
    far_count,
):
    count, _, clusters, panels = basis.shape
    ranks = source_basis.shape[2]
    slots = coupling.shape[1]
    owners = lax.axis_size(CL)
    width = clusters * ranks
    packed = 2 * LANES

    sent, current, targets, sources = pl.pallas_call(
        expand_kernel,
        in_specs=[HBM] * 4,
        out_specs=[VMEM] * 4,
        out_shape=[
            bf16(owners, width // LANES, LANES),
            pltpu.VMEM((clusters, panels), jnp.bfloat16),
            pltpu.VMEM((1, LANES), jnp.int32),
            pltpu.VMEM(far_source.shape, jnp.int32),
        ],
        scratch_shapes=[
            pltpu.VMEM((clusters, panels), jnp.float32),
            pltpu.VMEM((clusters, ranks, panels), jnp.bfloat16),
            pltpu.SemaphoreType.DMA((4,)),
        ],
        name="expand",
    )(basis, source_basis, far_target, far_source)
    expansions = exchange(sent, CL)
    current = pl.pallas_call(
        relay_kernel,
        in_specs=[VMEM, ANY],
        out_specs=VMEM,
        out_shape=bf16(clusters, panels),
        compiler_params=SMALL,
        cost_estimate=pl.CostEstimate(flops=0, bytes_accessed=1 << 26, transcendentals=0),
        name="relay",
    )(current, sent)
    other = swapped(current, 1)
    pair = swapped(current, 0)

    sent, held = pl.pallas_call(
        lambda *refs: far_kernel(clusters, owners, *refs),
        in_specs=[SMEM, SMEM, SMEM, VMEM, VMEM, VMEM],
        out_specs=[VMEM, VMEM],
        out_shape=[bf16(owners, width // LANES, LANES), bf16(clusters, panels)],
        compiler_params=SMALL,
        name="far",
    )(sources, targets, far_count, expansions, coupling, current)
    arrived = exchange(sent, CL)

    near = pl.pallas_call(
        near_kernel,
        in_specs=[SMEM, VMEM, VMEM, VMEM, VMEM],
        out_specs=VMEM,
        out_shape=f32(clusters, panels),
        scratch_shapes=[pltpu.VMEM((3 * clusters, panels), jnp.float32)],
        compiler_params=SMALL,
        name="near",
    )(near_list[0].T, pair, held, other, near_blocks)
    gram = pl.pallas_call(
        gram_kernel,
        in_specs=[VMEM, ANY],
        out_specs=VMEM,
        out_shape=f32(1, packed),
        compiler_params=SMALL,
        name="gram",
    )(basis, near)
    image, sent = pl.pallas_call(
        lambda *refs: image_kernel(owners, *refs),
        in_specs=[VMEM] * 5,
        out_specs=[VMEM] * 2,
        out_shape=[f32(clusters, panels), f32(lax.axis_size(ROW), 1, packed)],
        compiler_params=SMALL,
        name="image",
    )(basis, target_basis, arrived, near, gram)
    sent = pl.pallas_call(
        total_kernel,
        in_specs=[VMEM],
        out_specs=VMEM,
        out_shape=f32(lax.axis_size(COLUMN), 1, packed),
        compiler_params=SMALL,
        name="total",
    )(exchange(sent, ROW))
    all_panels = float(owners * lax.axis_size("grp") * clusters * panels)
    next_vector, hessenberg = pl.pallas_call(
        lambda *refs: final_kernel(all_panels, *refs),
        in_specs=[VMEM] * 3,
        out_specs=[VMEM] * 2,
        out_shape=[f32(1, clusters, panels), f32(1, count + 1)],
        compiler_params=SMALL,
        name="final",
    )(basis, image, exchange(sent, COLUMN))
    return (next_vector, hessenberg.reshape(count + 1))


def solution(mesh):
    torus = Mesh(mesh.devices.reshape(8, 8, 2, mesh.shape["grp"]), (*CL, "grp"))
    in_specs = (
        P(None, "grp", CL, None),
        P("grp", CL, None, None, None),
        P("grp", CL, None),
        P("grp", CL, None, None),
        P("grp", CL, None, None),
        P("grp", CL, None),
        P("grp", None),
        P("grp", CL),
        P("grp", CL),
    )
    return jax.shard_map(
        on_device,
        mesh=torus,
        in_specs=in_specs,
        out_specs=(P("grp", CL, None), P()),
        check_vma=False,
    )
```

```python
import jax
import jax.numpy as jnp
from jax import lax
from jax.experimental import pallas as pl
from jax.experimental.pallas import tpu as pltpu
from jax.sharding import Mesh
from jax.sharding import PartitionSpec as P

CL = ("z", "x", "core")
ROW = ("x", "core")
COLUMN = ("z", "grp")
HIGHEST = lax.Precision.HIGHEST
LANES = 128
SHARERS = 8
FIRST, LAST = -2, 3

SMALL = pltpu.CompilerParams(vmem_limit_bytes=4 * 1024 * 1024)
VMEM = pl.BlockSpec(memory_space=pltpu.VMEM)
ANY = pl.BlockSpec(memory_space=pl.ANY)
HBM = pl.BlockSpec(memory_space=pltpu.HBM)
SMEM = pl.BlockSpec(memory_space=pltpu.SMEM)


def iota(shape, dim):
    return lax.broadcasted_iota(jnp.int32, shape, dim)


def dot(a, b, contract=((1,), (0,)), precision=None):
    return lax.dot_general(
        a, b, (contract, ((), ())), precision=precision, preferred_element_type=jnp.float32
    )


def ones_where(mask, dtype):
    return jnp.where(mask, 1.0, 0.0).astype(dtype)


def position():
    return lax.axis_index("z") * 16 + lax.axis_index("x") * 2 + lax.axis_index("core")


def relay_kernel(tile_ref, after_ref, relayed_ref):
    relayed_ref[...] = tile_ref[...]


def expand_kernel(
    basis_ref,
    source_ref,
    target_ref,
    slot_ref,
    sent_ref,
    current_ref,
    window_ref,
    sources_ref,
    tile_ref,
    matrix_ref,
    semaphores,
):
    count, _, clusters, panels = basis_ref.shape
    ranks = source_ref.shape[2]
    width = clusters * ranks
    first = pl.multiple_of(position() // SHARERS * LANES, LANES)
    copies = [
        pltpu.make_async_copy(basis_ref.at[count - 1, 0], tile_ref, semaphores.at[0]),
        pltpu.make_async_copy(source_ref.at[0], matrix_ref, semaphores.at[1]),
        pltpu.make_async_copy(target_ref.at[:, pl.ds(first, LANES)], window_ref, semaphores.at[2]),
        pltpu.make_async_copy(slot_ref, sources_ref, semaphores.at[3]),
    ]
    for copy in copies:
        copy.start()
    copies[0].wait()
    current = tile_ref[...].astype(jnp.bfloat16)
    current_ref[...] = current
    copies[1].wait()
    every = dot(current, matrix_ref[...].reshape(width, panels), ((1,), (1,)))
    own = iota((clusters, width), 1) // ranks == iota((clusters, width), 0)
    row = jnp.sum(jnp.where(own, every, 0.0), axis=0, keepdims=True)
    pieces = [row[:, i : i + LANES] for i in range(0, width, LANES)]
    tile = jnp.concatenate(pieces, axis=0).astype(jnp.bfloat16)
    sent_ref[...] = jnp.broadcast_to(tile[None], sent_ref.shape)
    copies[2].wait()
    copies[3].wait()


def far_kernel(
    clusters,
    owners,
    source_ref,
    target_ref,
    count_ref,
    expansion_ref,
    coupling_ref,
    current_ref,
    after_ref,
    sent_ref,
    held_ref,
):
    held_ref[...] = current_ref[...]
    slots = coupling_ref.shape[1]
    width = expansion_ref.shape[1] * LANES
    ranks = width // clusters
    groups = LANES // ranks
    parts = ranks // groups
    me = position()
    lane_cluster = iota((1, width), 1) // ranks
    tile = expansion_ref.shape[1:]
    place = iota(tile, 0) * groups + iota(tile, 1) // ranks
    picked, targets = [], []
    for b in range(slots):
        source = source_ref[0, b]
        rows = expansion_ref[source // clusters].astype(jnp.float32)
        rows = jnp.where(place == source % clusters, rows, 0.0)
        picked.append(jnp.sum(rows, axis=0, keepdims=True))
        target = jnp.where(b < count_ref[0, 0], target_ref[0, lax.rem(me, SHARERS) * slots + b], -1)
        targets.append(jnp.full((1, width), target, jnp.int32))
    picked = jnp.concatenate(picked, axis=0).astype(jnp.bfloat16)
    targets = jnp.concatenate(targets, axis=0)
    spread = iota((LANES, LANES), 0) % ranks == iota((LANES, LANES), 1) % ranks
    vector = dot(picked, ones_where(spread, jnp.bfloat16))
    coupling = coupling_ref[0].astype(jnp.float32)
    high, low = [], []
    for q in range(parts):
        product = coupling[:, q * LANES : (q + 1) * LANES] * vector
        top = product.astype(jnp.bfloat16)
        high.append(top)
        low.append((product - top.astype(jnp.float32)).astype(jnp.bfloat16))
    gather = iota((LANES, width), 0) // ranks == iota((LANES, width), 1) % groups
    sums = dot(jnp.concatenate(high + low, axis=0), ones_where(gather, jnp.bfloat16))
    part = (iota((slots, width), 1) % ranks) // groups
    term = jnp.zeros((slots, width), jnp.float32)
    for q in range(parts):
        value = sums[q * slots : (q + 1) * slots] + sums[(parts + q) * slots : (parts + q + 1) * slots]
        term = jnp.where(part == q, value, term)
    sent_ref[...] = jnp.zeros_like(sent_ref)

    def send(owner):
        mine = targets == owner * clusters + lane_cluster
        row = jnp.sum(jnp.where(mine, term, 0.0), axis=0, keepdims=True)
        pieces = [row[:, i : i + LANES] for i in range(0, width, LANES)]
        sent_ref[owner] = jnp.concatenate(pieces, axis=0).astype(jnp.bfloat16)

    for step in range(FIRST, LAST + 1):
        owner = me + step

        @pl.when(jnp.logical_and(owner >= 0, owner < owners))
        def _():
            send(owner)

    send(lax.rem(me + owners // 2, owners))


def kept(count):
    return count * (count // 2 + 1)


def near_kernel(list_ref, pair_ref, held_ref, other_ref, blocks_ref, near_ref, window_ref):
    _, clusters, blocks, panels, _ = blocks_ref.shape
    for i, tile in enumerate((pair_ref, held_ref, other_ref)):
        window_ref[i * clusters : (i + 1) * clusters] = tile[...].astype(jnp.float32)
    even = lax.axis_index("core") == 0
    for t in range(clusters):
        rows = []
        for k in range(blocks):
            index = list_ref[k, t]
            mirrored = (2 - index // clusters) * clusters + index % clusters
            rows.append(window_ref[pl.ds(jnp.where(even, mirrored, index), 1), :])
        rows.append(jnp.zeros((8 - blocks, panels), jnp.float32))
        vectors = jnp.concatenate(rows, axis=0).astype(jnp.bfloat16)
        matrix = blocks_ref[0, t].reshape(blocks * panels, panels)
        every = dot(vectors, matrix, ((1,), (1,)))
        total = every[0:1, :panels]
        for k in range(1, blocks):
            total = total + every[k : k + 1, k * panels : (k + 1) * panels]
        near_ref[t : t + 1, :] = total


def gram_kernel(basis_ref, after_ref, gram_ref):
    count, _, clusters, _ = basis_ref.shape
    gram = jnp.zeros((count, count), jnp.float32)
    for c in range(clusters):
        rows = basis_ref[:, 0, c, :]
        gram = gram + dot(rows, rows, ((1,), (1,)), HIGHEST)
    lane = iota((count, gram_ref.shape[1]), 1)
    row = iota((count, gram_ref.shape[1]), 0)
    pick = jnp.logical_and((lane + lane // count) % count == row, lane < kept(count))
    rows = dot(gram, ones_where(pick, jnp.float32), precision=HIGHEST)
    gram_ref[...] = jnp.sum(jnp.where(lane % count == row, rows, 0.0), axis=0, keepdims=True)


def image_kernel(owners, basis_ref, target_ref, arrived_ref, near_ref, gram_ref, image_ref, sent_ref):
    count = basis_ref.shape[0]
    clusters, panels = near_ref.shape
    ranks = target_ref.shape[2]
    width = clusters * ranks
    me = position()
    coupled = arrived_ref[lax.rem(me + owners // 2, owners)].astype(jnp.float32)
    for step in range(-LAST, -FIRST + 1):
        owner = me + step
        inside = jnp.logical_and(owner >= 0, owner < owners)
        value = arrived_ref[jnp.clip(owner, 0, owners - 1)].astype(jnp.float32)
        coupled = coupled + jnp.where(inside, value, 0.0)
    coupled = jnp.concatenate([coupled[i : i + 1] for i in range(coupled.shape[0])], axis=1)
    own = iota((clusters, width), 1) // ranks == iota((clusters, width), 0)
    spread = jnp.where(own, coupled, 0.0).astype(jnp.bfloat16)
    far = dot(spread, target_ref[0].reshape(width, panels))
    image = 0.5 * basis_ref[count - 1, 0] + near_ref[...] + far
    image_ref[...] = image
    first = kept(count) % LANES
    rows = [jnp.zeros((first, panels), jnp.float32)]
    rows += [jnp.sum(basis_ref[k, 0] * image, axis=0, keepdims=True) for k in range(count)]
    rows.append(jnp.sum(image * image, axis=0, keepdims=True))
    rows.append(jnp.zeros((LANES - first - count - 1, panels), jnp.float32))
    products = dot(
        jnp.ones((8, panels), jnp.float32), jnp.concatenate(rows, axis=0), ((1,), (1,)), HIGHEST
    )
    gram = gram_ref[...]
    row = jnp.concatenate([gram[:, :LANES], gram[:, LANES:] + products[:1]], axis=1)
    sent_ref[...] = jnp.broadcast_to(row[None], sent_ref.shape)


def total_kernel(arrived_ref, sent_ref):
    sent_ref[...] = jnp.broadcast_to(
        jnp.sum(arrived_ref[...], axis=0, keepdims=True), sent_ref.shape
    )


def final_kernel(all_panels, basis_ref, image_ref, arrived_ref, next_ref, hessenberg_ref):
    count = basis_ref.shape[0]
    first = kept(count) % LANES
    total = jnp.sum(arrived_ref[...], axis=0)
    products = total[:, LANES:]
    lane = iota((1, LANES), 1)
    inside = jnp.logical_and(lane >= first, lane < first + count)
    projection = jnp.where(inside, products / all_panels, 0.0)
    square = jnp.sum(jnp.where(lane == first + count, products, 0.0), axis=1, keepdims=True)
    index = iota((LANES, total.shape[1]), 1)
    which = iota((LANES, total.shape[1]), 0) - first
    many = jnp.broadcast_to(projection, (8, LANES))
    outer = dot(many, ones_where(index % count == which, jnp.float32), precision=HIGHEST)
    shifted = (index + index // count) % count == which
    inner = dot(many, ones_where(shifted, jnp.float32), precision=HIGHEST)
    diagonal = iota(total.shape, 1) // count
    once = jnp.logical_or(diagonal == 0, diagonal == count // 2)
    gram = jnp.where(diagonal <= count // 2, total * jnp.where(once, 1.0, 2.0), 0.0)
    squares = (
        square
        - 2.0 * jnp.sum(projection * products, axis=1, keepdims=True)
        + jnp.sum(gram * outer[:1] * inner[:1], axis=1, keepdims=True)
    )
    new_norm = jnp.sqrt(squares / all_panels + 1e-06)
    remainder = image_ref[...]
    for k in range(count):
        remainder = remainder - projection[:, first + k : first + k + 1] * basis_ref[k, 0]
    next_ref[0] = remainder / new_norm
    column = jnp.where(lane == first + count, new_norm, projection)
    hessenberg_ref[...] = column[:, first : first + count + 1]


def exchange(rows, axes):
    return lax.all_to_all(rows, axes, 0, 0)


def swapped(value, first):
    count = lax.axis_size(CL)
    route = []
    for i in range(first, count - 1, 2):
        route += [(i, i + 1), (i + 1, i)]
    return lax.ppermute(value, CL, route)


def f32(*shape):
    return jax.ShapeDtypeStruct(shape, jnp.float32)


def bf16(*shape):
    return jax.ShapeDtypeStruct(shape, jnp.bfloat16)


def on_device(
    basis,
    near_blocks,
    near_list,
    source_basis,
    target_basis,
    coupling,
    far_target,
    far_source,
    far_count,
):
    count, _, clusters, panels = basis.shape
    ranks = source_basis.shape[2]
    slots = coupling.shape[1]
    owners = lax.axis_size(CL)
    width = clusters * ranks
    packed = 2 * LANES

    sent, current, targets, sources = pl.pallas_call(
        expand_kernel,
        in_specs=[HBM] * 4,
        out_specs=[VMEM] * 4,
        out_shape=[
            bf16(owners, width // LANES, LANES),
            pltpu.VMEM((clusters, panels), jnp.bfloat16),
            pltpu.VMEM((1, LANES), jnp.int32),
            pltpu.VMEM(far_source.shape, jnp.int32),
        ],
        scratch_shapes=[
            pltpu.VMEM((clusters, panels), jnp.float32),
            pltpu.VMEM((clusters, ranks, panels), jnp.bfloat16),
            pltpu.SemaphoreType.DMA((4,)),
        ],
        name="expand",
    )(basis, source_basis, far_target, far_source)
    expansions = exchange(sent, CL)
    current = pl.pallas_call(
        relay_kernel,
        in_specs=[VMEM, ANY],
        out_specs=VMEM,
        out_shape=bf16(clusters, panels),
        compiler_params=SMALL,
        cost_estimate=pl.CostEstimate(flops=0, bytes_accessed=1 << 26, transcendentals=0),
        name="relay",
    )(current, sent)
    other = swapped(current, 1)
    pair = swapped(current, 0)

    sent, held = pl.pallas_call(
        lambda *refs: far_kernel(clusters, owners, *refs),
        in_specs=[SMEM, SMEM, SMEM, VMEM, VMEM, VMEM, ANY],
        out_specs=[VMEM, VMEM],
        out_shape=[bf16(owners, width // LANES, LANES), bf16(clusters, panels)],
        compiler_params=SMALL,
        name="far",
    )(sources, targets, far_count, expansions, coupling, current, other)
    arrived = exchange(sent, CL)

    near = pl.pallas_call(
        near_kernel,
        in_specs=[SMEM, VMEM, VMEM, VMEM, VMEM],
        out_specs=VMEM,
        out_shape=f32(clusters, panels),
        scratch_shapes=[pltpu.VMEM((3 * clusters, panels), jnp.float32)],
        compiler_params=SMALL,
        name="near",
    )(near_list[0].T, pair, held, other, near_blocks)
    gram = pl.pallas_call(
        gram_kernel,
        in_specs=[VMEM, ANY],
        out_specs=VMEM,
        out_shape=f32(1, packed),
        compiler_params=SMALL,
        name="gram",
    )(basis, held)
    image, sent = pl.pallas_call(
        lambda *refs: image_kernel(owners, *refs),
        in_specs=[VMEM] * 5,
        out_specs=[VMEM] * 2,
        out_shape=[f32(clusters, panels), f32(lax.axis_size(ROW), 1, packed)],
        compiler_params=SMALL,
        name="image",
    )(basis, target_basis, arrived, near, gram)
    sent = pl.pallas_call(
        total_kernel,
        in_specs=[VMEM],
        out_specs=VMEM,
        out_shape=f32(lax.axis_size(COLUMN), 1, packed),
        compiler_params=SMALL,
        name="total",
    )(exchange(sent, ROW))
    all_panels = float(owners * lax.axis_size("grp") * clusters * panels)
    next_vector, hessenberg = pl.pallas_call(
        lambda *refs: final_kernel(all_panels, *refs),
        in_specs=[VMEM] * 3,
        out_specs=[VMEM] * 2,
        out_shape=[f32(1, clusters, panels), f32(1, count + 1)],
        compiler_params=SMALL,
        name="final",
    )(basis, image, exchange(sent, COLUMN))
    return (next_vector, hessenberg.reshape(count + 1))


def solution(mesh):
    torus = Mesh(mesh.devices.reshape(8, 8, 2, mesh.shape["grp"]), (*CL, "grp"))
    in_specs = (
        P(None, "grp", CL, None),
        P("grp", CL, None, None, None),
        P("grp", CL, None),
        P("grp", CL, None, None),
        P("grp", CL, None, None),
        P("grp", CL, None),
        P("grp", None),
        P("grp", CL),
        P("grp", CL),
    )
    return jax.shard_map(
        on_device,
        mesh=torus,
        in_specs=in_specs,
        out_specs=(P("grp", CL, None), P()),
        check_vma=False,
    )
```
